128 devices in a mesh: ctx: 32 (over z, x, core), head: 4 (over y).
Axes of the slice: x: 4, y: 4, z: 4, core: 2. Of those that a mesh axis runs over, the one named last changes fastest.
Arguments:
- tokens: bfloat16 [8192, 3072], P('ctx', 'head'), may hold values from -6 to 6
- query_key_value_weight: bfloat16 [3, 3072, 4096], P(None, None, 'head'), may hold values from -0.109375 to 0.109375
- output_weight: bfloat16 [4096, 3072], P('head'), may hold values from -0.09375 to 0.09375
- input_down_weights: bfloat16 [3, 3072, 16], P(None, 'head'), may hold values from -0.109375 to 0.109375
- input_up_weights: bfloat16 [3, 16, 4096], P(None, None, 'head'), may hold values from -1.5 to 1.5
- output_down_weight: bfloat16 [4096, 16], P('head'), may hold values from -0.09375 to 0.09375
- output_up_weight: bfloat16 [16, 3072], P(None, 'head'), may hold values from -1.5 to 1.5
- cotangent: bfloat16 [8192, 3072], P('ctx', 'head'), may hold values from -6 to 6
Outputs:
- output: bfloat16 [8192, 3072], P('ctx', 'head')
- input_grad: bfloat16 [8192, 3072], P('ctx', 'head')
- grad_down_qkv: float32 [3, 3072, 16], P(None, 'head')
- grad_up_qkv: float32 [3, 16, 4096], P(None, None, 'head')
- grad_down_out: float32 [4096, 16], P('head')
- grad_up_out: float32 [16, 3072], P(None, 'head')
The draws below stay inside these ranges and needn't reach their ends.
All inputs are finite; a program needn't handle non-finite values.
Results may differ from the reference program's by a relative error of at most 0.029.
Values may be sent and summed in bfloat16 or wider, within the bound.
No kernel may reach another device: no remote copies, remote signals or barrier semaphores. Data moves between devices by JAX's collectives and lax.ppermute only.
A program may use at most 128 MiB of HBM per device.

```python
import jax
import jax.numpy as jnp
from jax import lax

D = 3072
HEADS = 32
HEAD_DIM = 128
RANK = 16
BLOCK = 256
TOKEN_COUNT = 8192


def levels(key, extent, shards, low, top_value):
    factor_of = 1.0
    for dim, parts in shards:
        draws = jax.random.uniform(jax.random.fold_in(jax.random.fold_in(key, 6), dim), (parts,), jnp.float32, low / len(shards), top_value / len(shards))
        factor_of = factor_of * jnp.repeat(jnp.exp(draws), extent[dim] // parts).reshape((-1,) + (1,) * (len(extent) - 1 - dim))
    return factor_of


def gaussian(key, dims, deviation, most, shards=(), dtype=jnp.bfloat16):
    level = levels(key, dims, shards, -0.22, 0.18) if shards else 1.0
    drawn = jax.random.normal(key, dims, jnp.float32) * deviation * level
    return jnp.minimum(jnp.maximum(drawn, -most), most).astype(dtype)


def setup_inputs(seed: int = 0) -> dict:
    splits = jax.random.split(jax.random.key(seed), 9)
    return {
        "tokens": gaussian(splits[0], (TOKEN_COUNT, D), 1.0, 6.0, ((0, 32), (1, 4))),
        "query_key_value_weight": gaussian(splits[1], (3, D, HEADS * HEAD_DIM), D ** -0.5, 0.109375, ((2, 4),)),
        "output_weight": gaussian(splits[2], (HEADS * HEAD_DIM, D), (HEADS * HEAD_DIM) ** -0.5, 0.09375, ((0, 4),)),
        "input_down_weights": gaussian(splits[3], (3, D, RANK), D ** -0.5, 0.109375, ((1, 4),)),
        "input_up_weights": gaussian(splits[4], (3, RANK, HEADS * HEAD_DIM), RANK ** -0.5, 1.5, ((2, 4),)),
        "output_down_weight": gaussian(splits[5], (HEADS * HEAD_DIM, RANK), (HEADS * HEAD_DIM) ** -0.5, 0.09375, ((0, 4),)),
        "output_up_weight": gaussian(splits[6], (RANK, D), RANK ** -0.5, 1.5, ((1, 4),)),
        "cotangent": gaussian(splits[7], (TOKEN_COUNT, D), 1.0, 6.0, ((0, 32), (1, 4))),
    }


adapter_scale = 0.5
epsilon = 1e-06

def causal_mask(length):
    position = jnp.arange(length)
    return position[:, None] >= position[None, :]

def forward_block(kv_state, blocks):
    q_block, k_block, v_block = blocks
    lower_mask = causal_mask(q_block.shape[0])
    scores = jnp.einsum('sjd,tjd->jst', q_block.astype(jnp.float32), k_block.astype(jnp.float32))
    scores = jnp.where(lower_mask[None], scores, 0.0).astype(jnp.bfloat16)
    held_state = kv_state.astype(jnp.bfloat16)
    raw_out = jnp.einsum('jst,tje->sje', scores.astype(jnp.float32), v_block.astype(jnp.float32))
    raw_out = raw_out + jnp.einsum('sjd,jde->sje', q_block.astype(jnp.float32), held_state.astype(jnp.float32))
    kv_state = kv_state + jnp.einsum('tjd,tje->jde', k_block.astype(jnp.float32), v_block.astype(jnp.float32))
    return (kv_state, (raw_out, held_state))

def backward_block(suffix_state, blocks):
    q_block, k_block, v_block, d_block, held_state = blocks
    lower_mask = causal_mask(q_block.shape[0])
    qf = q_block.astype(jnp.float32)
    kf = k_block.astype(jnp.float32)
    vf = v_block.astype(jnp.float32)
    dfl = d_block.astype(jnp.float32)
    scores = jnp.einsum('sjd,tjd->jst', qf, kf)
    scores = jnp.where(lower_mask[None], scores, 0.0).astype(jnp.bfloat16).astype(jnp.float32)
    d_scores = jnp.einsum('sje,tje->jst', dfl, vf)
    d_scores = jnp.where(lower_mask[None], d_scores, 0.0).astype(jnp.bfloat16).astype(jnp.float32)
    held_suffix = suffix_state.astype(jnp.bfloat16).astype(jnp.float32)
    held_prefix = held_state.astype(jnp.float32)
    d_query = jnp.einsum('jst,tjd->sjd', d_scores, kf) + jnp.einsum('sje,jde->sjd', dfl, held_prefix)
    d_key = jnp.einsum('jst,sjd->tjd', d_scores, qf) + jnp.einsum('tje,jde->tjd', vf, held_suffix)
    d_value = jnp.einsum('jst,sje->tje', scores, dfl) + jnp.einsum('tjd,jde->tje', kf, held_suffix)
    suffix_state = suffix_state + jnp.einsum('sjd,sje->jde', qf, dfl)
    return (suffix_state, (d_query.astype(jnp.bfloat16), d_key.astype(jnp.bfloat16), d_value.astype(jnp.bfloat16)))

def reference(tokens, query_key_value_weight, output_weight, input_down_weights, input_up_weights, output_down_weight, output_up_weight, cotangent):
    low_rank_rows = jnp.stack([jnp.dot(tokens, input_down_weights[projection_member], preferred_element_type=jnp.float32) for projection_member in range(3)]).astype(jnp.bfloat16)
    projected_rows = jnp.stack([jnp.dot(tokens, query_key_value_weight[projection_member], preferred_element_type=jnp.float32) + adapter_scale * jnp.dot(low_rank_rows[projection_member], input_up_weights[projection_member], preferred_element_type=jnp.float32) for projection_member in range(3)]).astype(jnp.bfloat16)
    blocked = projected_rows.reshape(3, TOKEN_COUNT // BLOCK, BLOCK, HEADS, HEAD_DIM)
    zero_state = jnp.zeros((HEADS, HEAD_DIM, HEAD_DIM), jnp.float32)
    final_state, (raw_out, held_state) = lax.scan(forward_block, zero_state, (blocked[0], blocked[1], blocked[2]))
    raw_out = raw_out.reshape(TOKEN_COUNT, HEADS, HEAD_DIM)
    root_mean = jnp.sqrt(lax.optimization_barrier(jnp.mean(raw_out * raw_out, axis=-1, keepdims=True)) + epsilon)
    normed = raw_out / root_mean
    attended_output = normed.astype(jnp.bfloat16).reshape(TOKEN_COUNT, HEADS * HEAD_DIM)
    middle_rank_rows = jnp.dot(attended_output, output_down_weight, preferred_element_type=jnp.float32).astype(jnp.bfloat16)
    output = (jnp.dot(attended_output, output_weight, preferred_element_type=jnp.float32) + adapter_scale * jnp.dot(middle_rank_rows, output_up_weight, preferred_element_type=jnp.float32)).astype(jnp.bfloat16)
    backward_middle = jnp.dot(cotangent, output_up_weight.T, preferred_element_type=jnp.float32).astype(jnp.bfloat16)
    attended_gradient = jnp.dot(cotangent, output_weight.T, preferred_element_type=jnp.float32) + adapter_scale * jnp.dot(backward_middle, output_down_weight.T, preferred_element_type=jnp.float32)
    attended_gradient = attended_gradient.reshape(TOKEN_COUNT, HEADS, HEAD_DIM)
    d_raw = ((attended_gradient - normed * lax.optimization_barrier(jnp.mean(attended_gradient * normed, axis=-1, keepdims=True))) / root_mean).astype(jnp.bfloat16)
    d_blocks = d_raw.reshape(TOKEN_COUNT // BLOCK, BLOCK, HEADS, HEAD_DIM)
    last_state, grad_parts = lax.scan(backward_block, zero_state, (blocked[0], blocked[1], blocked[2], d_blocks, held_state), reverse=True)
    d_proj = jnp.stack(grad_parts).reshape(3, TOKEN_COUNT, HEADS * HEAD_DIM)
    backward_low_rank = jnp.stack([jnp.dot(d_proj[projection_member], input_up_weights[projection_member].T, preferred_element_type=jnp.float32) for projection_member in range(3)]).astype(jnp.bfloat16)
    gradient_total = jnp.zeros((TOKEN_COUNT, D), jnp.float32)
    for projection_member in range(3):
        gradient_total = gradient_total + jnp.dot(d_proj[projection_member], query_key_value_weight[projection_member].T, preferred_element_type=jnp.float32)
        gradient_total = gradient_total + adapter_scale * jnp.dot(backward_low_rank[projection_member], input_down_weights[projection_member].T, preferred_element_type=jnp.float32)
    input_grad = gradient_total.astype(jnp.bfloat16)
    scale_factor = adapter_scale * TOKEN_COUNT ** (-0.5)
    grad_down_qkv = scale_factor * jnp.stack([jnp.dot(tokens.T, backward_low_rank[projection_member], preferred_element_type=jnp.float32) for projection_member in range(3)])
    grad_up_qkv = scale_factor * jnp.stack([jnp.dot(low_rank_rows[projection_member].T, d_proj[projection_member], preferred_element_type=jnp.float32) for projection_member in range(3)])
    grad_down_out = scale_factor * jnp.dot(attended_output.T, backward_middle, preferred_element_type=jnp.float32)
    grad_up_out = scale_factor * jnp.dot(middle_rank_rows.T, cotangent, preferred_element_type=jnp.float32)
    return (output, input_grad, grad_down_qkv, grad_up_qkv, grad_down_out, grad_up_out)
```

```python
import functools

import jax
import jax.numpy as jnp
from jax import lax
from jax.experimental import pallas as pl
from jax.experimental.pallas import tpu as pltpu
from jax.sharding import PartitionSpec as P

HEAD_DIM = 128
RANK = 16
PAIR = 2 * HEAD_DIM
adapter_scale = 0.5
epsilon = 1e-06
bf16 = jnp.bfloat16
f32 = jnp.float32
VMEM_BYTES = 24 * 2**20

NN = (((1,), (0,)), ((), ()))
NT = (((1,), (1,)), ((), ()))
TN = (((0,), (0,)), ((), ()))


def mm(a, b, dims=NN):
    return lax.dot_general(a, b, dims, preferred_element_type=f32)


def call(kernel, grid, in_specs, out_specs, out_shape, flops, moved, prefetch=0):
    return pl.pallas_call(
        kernel,
        grid_spec=pltpu.PrefetchScalarGridSpec(
            num_scalar_prefetch=prefetch, grid=grid, in_specs=in_specs, out_specs=out_specs
        ),
        out_shape=out_shape,
        compiler_params=pltpu.CompilerParams(
            dimension_semantics=("arbitrary",) * len(grid), vmem_limit_bytes=VMEM_BYTES
        ),
        cost_estimate=pl.CostEstimate(flops=flops, bytes_accessed=moved, transcendentals=0),
    )


def whole(shape):
    return pl.BlockSpec(shape, lambda *_: (0,) * len(shape))


def struct(shape, dtype):
    return jax.ShapeDtypeStruct(shape, dtype)


def project_kernel(chunks, with_sum, idx_ref, *refs):
    toks, weights = refs[:chunks], refs[chunks : 2 * chunks]
    total_ref = refs[2 * chunks] if with_sum else None
    out_ref = refs[-1]
    for m in range(3):
        total = mm(toks[0][...], weights[0][m])
        for c in range(1, chunks):
            total = total + mm(toks[c][...], weights[c][m])
        if with_sum:
            total = total + total_ref[m]
        out_ref[m] = total


def weight_specs(count, width):
    return [
        pl.BlockSpec((3, width, PAIR), functools.partial(lambda c, i, idx: (0, idx[c], i), c))
        for c in range(count)
    ]


def project(idx, toks, weight, total=None):
    count = len(toks)
    rows, width = toks[0].shape
    cols = weight.shape[2]
    tile = pl.BlockSpec((3, rows, PAIR), lambda i, idx: (0, 0, i))
    in_specs = [whole((rows, width))] * count + weight_specs(count, width)
    operands = list(toks) + [weight] * count
    if total is not None:
        in_specs.append(tile)
        operands.append(total)
    return call(
        functools.partial(project_kernel, count, total is not None),
        (cols // PAIR,),
        in_specs,
        tile,
        struct((3, rows, cols), f32),
        6 * rows * width * cols * count,
        6 * width * cols * count + 24 * rows * cols,
        prefetch=1,
    )(idx, *operands)


def project_last_kernel(idx_ref, tok_ref, weight_ref, total_ref, low_ref, up_ref, out_ref, state_ref):
    parts = []
    for m in range(3):
        total = mm(tok_ref[...], weight_ref[m]) + total_ref[m]
        total = total + adapter_scale * mm(low_ref[m], up_ref[m])
        part = total.astype(bf16)
        out_ref[m] = part
        parts.append(part)
    for h in range(2):
        at = slice(h * HEAD_DIM, (h + 1) * HEAD_DIM)
        state_ref[h] = mm(parts[1][:, at], parts[2][:, at], TN)


def project_last(idx, tok, weight, total, low, up):
    rows, width = tok.shape
    cols = weight.shape[2]
    tile = pl.BlockSpec((3, rows, PAIR), lambda i, idx: (0, 0, i))
    return call(
        project_last_kernel,
        (cols // PAIR,),
        [whole((rows, width))]
        + weight_specs(1, width)
        + [tile, whole((3, rows, RANK)), pl.BlockSpec((3, RANK, PAIR), lambda i, idx: (0, 0, i))],
        [tile, pl.BlockSpec((2, HEAD_DIM, HEAD_DIM), lambda i, idx: (i, 0, 0))],
        [struct((3, rows, cols), bf16), struct((cols // HEAD_DIM, HEAD_DIM, HEAD_DIM), f32)],
        6 * rows * width * cols,
        6 * width * cols + 18 * rows * cols,
        prefetch=1,
    )(idx, tok, weight, total, low, up)


def attended_gradient_kernel(idx_ref, *refs):
    cots, weights = refs[:4], refs[4:8]
    back_ref, down_ref, out_ref = refs[8:]
    total = adapter_scale * mm(back_ref[...], down_ref[...])
    for c in range(4):
        total = total + mm(cots[c][...], weights[c][...], NT)
    out_ref[...] = total


def attended_gradient(idx, cots, weight, back_mid, down_out):
    rows, width = cots[0].shape
    cols = weight.shape[0]
    return call(
        attended_gradient_kernel,
        (cols // PAIR,),
        [whole((rows, width))] * 4
        + [
            pl.BlockSpec((PAIR, width), functools.partial(lambda c, i, idx: (i, idx[c]), c))
            for c in range(4)
        ]
        + [whole((rows, RANK)), pl.BlockSpec((RANK, PAIR), lambda i, idx: (0, i))],
        pl.BlockSpec((rows, PAIR), lambda i, idx: (0, i)),
        struct((rows, cols), f32),
        8 * rows * width * cols,
        8 * width * cols + 8 * rows * width + 4 * rows * cols,
        prefetch=1,
    )(idx, *cots, *([weight] * 4), back_mid, down_out)


def lower_mask(rows):
    s = lax.broadcasted_iota(jnp.int32, (rows, rows), 0)
    t = lax.broadcasted_iota(jnp.int32, (rows, rows), 1)
    return s >= t


def forward_kernel(
    qkv_ref, held_ref, grad_ref, back_ref, down_ref, att_ref, draw_ref, state_ref, mid_ref, gdown_ref
):
    rows = att_ref.shape[0]
    mask = lower_mask(rows)

    @pl.when(pl.program_id(0) == 0)
    def _():
        mid_ref[...] = jnp.zeros_like(mid_ref)

    for h in range(2):
        at = slice(h * HEAD_DIM, (h + 1) * HEAD_DIM)
        q, k, v = (qkv_ref[m, :, at] for m in range(3))
        scores = jnp.where(mask, mm(q, k, NT), 0.0).astype(bf16)
        raw = mm(scores, v) + mm(q, held_ref[h])
        inverse = 1.0 / jnp.sqrt(jnp.mean(raw * raw, axis=-1, keepdims=True) + epsilon)
        normed = raw * inverse
        att = normed.astype(bf16)
        grad = grad_ref[:, at]
        along = jnp.mean(grad * normed, axis=-1, keepdims=True)
        draw = ((grad - normed * along) * inverse).astype(bf16)
        att_ref[:, at] = att
        draw_ref[:, at] = draw
        state_ref[h] = mm(q, draw, TN)
        gdown_ref[h] = mm(back_ref[...], att)
        mid_ref[...] += mm(att, down_ref[:, at], NT)


def forward_heads(qkv, held, grad, back_mid_t, down_out):
    _, rows, cols = qkv.shape
    heads = cols // HEAD_DIM
    tile = pl.BlockSpec((rows, PAIR), lambda i: (0, i))
    state = pl.BlockSpec((2, HEAD_DIM, HEAD_DIM), lambda i: (i, 0, 0))
    return call(
        forward_kernel,
        (cols // PAIR,),
        [
            pl.BlockSpec((3, rows, PAIR), lambda i: (0, 0, i)),
            state,
            tile,
            whole((RANK, rows)),
            pl.BlockSpec((RANK, PAIR), lambda i: (0, i)),
        ],
        [
            tile,
            tile,
            state,
            whole((rows, RANK)),
            pl.BlockSpec((2, RANK, HEAD_DIM), lambda i: (i, 0, 0)),
        ],
        [
            struct((rows, cols), bf16),
            struct((rows, cols), bf16),
            struct((heads, HEAD_DIM, HEAD_DIM), f32),
            struct((rows, RANK), f32),
            struct((heads, RANK, HEAD_DIM), f32),
        ],
        4 * rows * cols * (2 * rows + 2 * HEAD_DIM),
        14 * rows * cols,
    )(qkv, held, grad, back_mid_t, down_out)


def within_kernel(
    qkv_ref, held_ref, draw_ref, low_ref, up_ref, dq_ref, dk_ref, dv_ref, back_ref, gup_ref
):
    rows = draw_ref.shape[0]
    mask = lower_mask(rows)

    @pl.when(pl.program_id(0) == 0)
    def _():
        back_ref[...] = jnp.zeros_like(back_ref)

    for h in range(2):
        at = slice(h * HEAD_DIM, (h + 1) * HEAD_DIM)
        q, k, v = (qkv_ref[m, :, at] for m in range(3))
        draw = draw_ref[:, at]
        scores = jnp.where(mask, mm(q, k, NT), 0.0).astype(bf16)
        dscores = jnp.where(mask, mm(draw, v, NT), 0.0).astype(bf16)
        dq = (mm(dscores, k) + mm(draw, held_ref[h], NT)).astype(bf16)
        dq_ref[:, at] = dq
        dk_ref[:, at] = mm(dscores, q, TN)
        dv_ref[:, at] = mm(scores, draw, TN)
        back_ref[...] += mm(dq, up_ref[:, at], NT)
        gup_ref[h] = mm(low_ref[...], dq)


def within_block(qkv, held, draw, low_t, up):
    _, rows, cols = qkv.shape
    heads = cols // HEAD_DIM
    tile = pl.BlockSpec((rows, PAIR), lambda i: (0, i))
    return call(
        within_kernel,
        (cols // PAIR,),
        [
            pl.BlockSpec((3, rows, PAIR), lambda i: (0, 0, i)),
            pl.BlockSpec((2, HEAD_DIM, HEAD_DIM), lambda i: (i, 0, 0)),
            tile,
            whole((RANK, rows)),
            pl.BlockSpec((RANK, PAIR), lambda i: (0, i)),
        ],
        [
            tile,
            tile,
            tile,
            whole((rows, RANK)),
            pl.BlockSpec((2, RANK, HEAD_DIM), lambda i: (i, 0, 0)),
        ],
        [
            struct((rows, cols), bf16),
            struct((rows, cols), f32),
            struct((rows, cols), f32),
            struct((rows, RANK), f32),
            struct((heads, RANK, HEAD_DIM), f32),
        ],
        4 * rows * cols * (5 * rows + HEAD_DIM),
        18 * rows * cols,
    )(qkv, held, draw, low_t, up)


def across_kernel(
    qkv_ref, suffix_ref, dk_ref, dv_ref, low_ref, up_ref, out_ref, back_ref, gup_ref
):
    @pl.when(pl.program_id(0) == 0)
    def _():
        back_ref[...] = jnp.zeros_like(back_ref)

    for h in range(2):
        at = slice(h * HEAD_DIM, (h + 1) * HEAD_DIM)
        k, v = qkv_ref[1, :, at], qkv_ref[2, :, at]
        held = suffix_ref[h]
        dk = (dk_ref[:, at] + mm(v, held, NT)).astype(bf16)
        dv = (dv_ref[:, at] + mm(k, held)).astype(bf16)
        for m, part in ((0, dk), (1, dv)):
            out_ref[m, :, at] = part
            back_ref[m] += mm(part, up_ref[m + 1, :, at], NT)
            gup_ref[m, h] = mm(low_ref[m + 1], part)


def across_blocks(qkv, suffix, dk, dv, low_t, up):
    _, rows, cols = qkv.shape
    heads = cols // HEAD_DIM
    tile = pl.BlockSpec((rows, PAIR), lambda i: (0, i))
    return call(
        across_kernel,
        (cols // PAIR,),
        [
            pl.BlockSpec((3, rows, PAIR), lambda i: (0, 0, i)),
            pl.BlockSpec((2, HEAD_DIM, HEAD_DIM), lambda i: (i, 0, 0)),
            tile,
            tile,
            whole((3, RANK, rows)),
            pl.BlockSpec((3, RANK, PAIR), lambda i: (0, 0, i)),
        ],
        [
            pl.BlockSpec((2, rows, PAIR), lambda i: (0, 0, i)),
            whole((2, rows, RANK)),
            pl.BlockSpec((2, 2, RANK, HEAD_DIM), lambda i: (0, i, 0, 0)),
        ],
        [
            struct((2, rows, cols), bf16),
            struct((2, rows, RANK), f32),
            struct((2, heads, RANK, HEAD_DIM), f32),
        ],
        8 * rows * cols * HEAD_DIM,
        18 * rows * cols,
    )(qkv, suffix, dk, dv, low_t, up)


def output_kernel(att_ref, weight_ref, out_ref):
    out_ref[0] = mm(att_ref[...], weight_ref[...]).astype(bf16)


def output_parts(att, weight, width):
    rows, cols = att.shape
    parts = weight.shape[1] // width
    return call(
        output_kernel,
        (parts,),
        [whole((rows, cols)), pl.BlockSpec((cols, width), lambda i: (0, i))],
        pl.BlockSpec((1, rows, width), lambda i: (i, 0, 0)),
        struct((parts, rows, width), bf16),
        2 * rows * cols * width * parts,
        2 * cols * width * parts,
    )(att, weight)


def input_kernel(idx_ref, dq_ref, dkv_ref, weight_ref, out_ref):
    total = mm(dq_ref[...], weight_ref[0], NT)
    for m in range(2):
        total = total + mm(dkv_ref[m], weight_ref[m + 1], NT)
    out_ref[...] = total.astype(out_ref.dtype)


def input_part(idx, dq, dkv, weight, width, dtype):
    rows, cols = dq.shape
    tiles = width // 256
    return call(
        input_kernel,
        (tiles,),
        [
            whole((rows, cols)),
            whole((2, rows, cols)),
            pl.BlockSpec((3, 256, cols), lambda i, idx: (0, idx[0] * tiles + i, 0)),
        ],
        pl.BlockSpec((rows, 256), lambda i, idx: (0, i)),
        struct((rows, width), dtype),
        6 * rows * cols * width,
        6 * cols * width + 6 * rows * cols,
        prefetch=1,
    )(idx, dq, dkv, weight)


def shift(array, by):
    n = lax.axis_size("head")
    return lax.ppermute(array, "head", [(i, (i + by) % n) for i in range(n)])


def sum_over_head(part):
    sent = part.astype(bf16)
    total = part
    for by in (2, 1, 3):
        total = total + shift(sent, by).astype(f32)
    return total


def swap_cores(array):
    n = lax.axis_size("ctx")
    return lax.ppermute(array, "ctx", [(i, i ^ 1) for i in range(n)])


def scan_states(state, reverse):
    n = lax.axis_size("ctx")
    chips = n // 2
    groups = [[core + 2 * chip for chip in range(chips)] for core in range(2)]
    heads = state.shape[0]
    half = heads // 2
    core = lax.axis_index("ctx") % 2
    first = core == (1 if reverse else 0)
    mine = lax.dynamic_slice_in_dim(state, core * half, half)
    given = lax.dynamic_slice_in_dim(state, (1 - core) * half, half)
    got = swap_cores(given.astype(bf16)).astype(f32)
    pair = (mine + got).astype(bf16).reshape(chips, -1, HEAD_DIM)
    every = lax.all_to_all(pair, "ctx", 0, 0, axis_index_groups=groups).astype(f32)
    before = jnp.cumsum(every, axis=0, dtype=f32)
    before = before[-1:] - before if reverse else before - every
    chip = lax.all_to_all(before.astype(bf16), "ctx", 0, 0, axis_index_groups=groups)
    chip = chip.reshape(mine.shape).astype(f32)
    own = jnp.where(first, chip, chip + got).astype(bf16)
    other = jnp.where(first, chip + mine, chip).astype(bf16)
    back = swap_cores(other)
    low = jnp.where(core == 0, own, back)
    high = jnp.where(core == 0, back, own)
    return jnp.concatenate([low, high])


def sum_over_ctx(parts):
    n = lax.axis_size("ctx")
    flat = parts.astype(bf16).reshape(n, -1, HEAD_DIM)
    every = lax.all_to_all(flat, "ctx", 0, 0).astype(f32)
    total = jnp.sum(every, axis=0).astype(bf16)
    spread = jnp.broadcast_to(total[None], flat.shape)
    return lax.all_to_all(spread, "ctx", 0, 0).reshape(parts.shape).astype(f32)


def blocks_of(rows):
    wide = rows.shape[-1] // HEAD_DIM
    return rows.reshape(RANK, wide, HEAD_DIM).transpose(1, 0, 2)


def rows_of(blocks):
    return blocks.transpose(1, 0, 2).reshape(RANK, -1)


def on_device(
    tokens,
    query_key_value_weight,
    output_weight,
    input_down_weights,
    input_up_weights,
    output_down_weight,
    output_up_weight,
    cotangent,
):
    rows, width = tokens.shape
    cols = query_key_value_weight.shape[2]
    heads = cols // HEAD_DIM
    me = lax.axis_index("head").astype(jnp.int32)
    parts = lax.axis_size("head")
    scale_factor = adapter_scale * (rows * lax.axis_size("ctx")) ** (-0.5)

    def index(*shifts):
        return jnp.stack([(me + s) % parts for s in shifts])

    down_t = input_down_weights.transpose(0, 2, 1).reshape(3 * RANK, width)
    down_out_t = output_down_weight.T

    from2, from1, from3 = shift(tokens, 2), shift(tokens, 1), shift(tokens, 3)

    low_part = mm(tokens, down_t, NT)
    back_part = mm(cotangent, output_up_weight, NT)
    low_all = sum_over_head(jnp.concatenate([low_part, back_part], axis=1)).astype(bf16)
    low = low_all[:, : 3 * RANK].reshape(rows, 3, RANK).transpose(1, 0, 2)
    low_t = low.transpose(0, 2, 1)
    back_mid = low_all[:, 3 * RANK :]

    total = project(index(0), [tokens], query_key_value_weight)
    total = project(index(-1, -3), [from1, from3], query_key_value_weight, total)
    qkv, kv_total = project_last(
        index(-2), from2, query_key_value_weight, total, low, input_up_weights
    )

    cots = [cotangent] + [shift(cotangent, s) for s in (2, 1, 3)]
    held = scan_states(kv_total, False)
    grad = attended_gradient(index(0, -2, -1, -3), cots, output_weight, back_mid, down_out_t)

    attended, d_raw, qd_total, mid_part, gdown_out = forward_heads(
        qkv, held, grad, back_mid.T, down_out_t
    )
    suffix = scan_states(qd_total, True)

    mid = sum_over_head(mid_part).astype(bf16)
    dq, dk_within, dv_within, back_q, gup_q = within_block(
        qkv, held, d_raw, low_t[0], input_up_weights[0]
    )
    out_parts = output_parts(attended, output_weight, width)
    out_every = lax.all_to_all(out_parts, "head", 0, 0)
    output = (
        jnp.sum(out_every.astype(f32), axis=0) + adapter_scale * mm(mid, output_up_weight)
    ).astype(bf16)
    gup_out = mm(mid, cotangent, TN)

    dkv, back_kv, gup_kv = across_blocks(
        qkv, suffix, dk_within, dv_within, low_t, input_up_weights
    )
    back_low = sum_over_head(jnp.concatenate([back_q, back_kv[0], back_kv[1]], axis=1)).astype(bf16)
    grad_parts = []
    for s in (2, 1, 3):
        part = input_part(index(s), dq, dkv, query_key_value_weight, width, bf16)
        grad_parts.append(shift(part, s))
    grad_sum = input_part(index(0), dq, dkv, query_key_value_weight, width, f32)
    grad_sum = grad_sum + adapter_scale * mm(back_low, down_t)
    for part in grad_parts:
        grad_sum = grad_sum + part.astype(f32)
    input_grad = grad_sum.astype(bf16)

    gdown = mm(back_low, tokens, TN).reshape(3, RANK, width)
    wide = width // HEAD_DIM
    sums = sum_over_ctx(
        jnp.concatenate(
            [blocks_of(gdown[m]) for m in range(3)]
            + [blocks_of(gup_out), gdown_out, gup_q, gup_kv[0], gup_kv[1]]
        )
    )
    sums = scale_factor * sums
    grad_down_qkv = jnp.stack(
        [rows_of(sums[m * wide : (m + 1) * wide]).T for m in range(3)]
    )
    at = 3 * wide
    grad_up_out = rows_of(sums[at : at + wide])
    at += wide
    grad_down_out = rows_of(sums[at : at + heads]).T
    at += heads
    grad_up_qkv = jnp.stack(
        [rows_of(sums[at + m * heads : at + (m + 1) * heads]) for m in range(3)]
    )
    return (output, input_grad, grad_down_qkv, grad_up_qkv, grad_down_out, grad_up_out)


def solution(mesh):
    return jax.shard_map(
        on_device,
        mesh=mesh,
        in_specs=(
            P("ctx", "head"),
            P(None, None, "head"),
            P("head", None),
            P(None, "head", None),
            P(None, None, "head"),
            P("head", None),
            P(None, "head"),
            P("ctx", "head"),
        ),
        out_specs=(
            P("ctx", "head"),
            P("ctx", "head"),
            P(None, "head", None),
            P(None, None, "head"),
            P("head", None),
            P(None, "head"),
        ),
        check_vma=False,
    )
```

```python
import functools

import jax
import jax.numpy as jnp
from jax import lax
from jax.experimental import pallas as pl
from jax.experimental.pallas import tpu as pltpu
from jax.sharding import PartitionSpec as P

HEAD_DIM = 128
RANK = 16
TILE = 256
LANES = 128
adapter_scale = 0.5
epsilon = 1e-06
bf16 = jnp.bfloat16
f32 = jnp.float32
VMEM_BYTES = 46 * 2**20

NN = (((1,), (0,)), ((), ()))
NT = (((1,), (1,)), ((), ()))
TN = (((0,), (0,)), ((), ()))

IN_HBM = pl.BlockSpec(memory_space=pltpu.HBM)
IN_VMEM = pl.BlockSpec(memory_space=pltpu.VMEM)
UNREAD = pl.BlockSpec(memory_space=pl.ANY)


def mm(a, b, dims=NN):
    return lax.dot_general(a, b, dims, preferred_element_type=f32)


def struct(shape, dtype):
    return jax.ShapeDtypeStruct(shape, dtype)


def call(kernel, specs, out_shape, flops, moved, scratch=(), aliases=None):
    many = isinstance(out_shape, (list, tuple))
    return pl.pallas_call(
        kernel,
        in_specs=specs,
        out_specs=[IN_VMEM] * len(out_shape) if many else IN_VMEM,
        out_shape=out_shape,
        scratch_shapes=list(scratch),
        input_output_aliases=aliases or {},
        compiler_params=pltpu.CompilerParams(vmem_limit_bytes=VMEM_BYTES),
        cost_estimate=pl.CostEstimate(flops=flops, bytes_accessed=moved, transcendentals=0),
    )


def member(shift):
    return lax.rem(lax.axis_index("head") + shift + 4, 4)


def first_core():
    return lax.rem(lax.axis_index("ctx"), 2) == 0


def fetch_columns(weight_ref, buffer, sems, chunk, width, base=0):
    copies = []
    for j in range(weight_ref.shape[2] // TILE):
        copies.append(
            pltpu.make_async_copy(
                weight_ref.at[
                    :, pl.ds(pl.multiple_of(chunk * width, width), width), pl.ds(j * TILE, TILE)
                ],
                buffer.at[base + j],
                sems.at[base + j],
            )
        )
    for copy in copies:
        copy.start()
    return copies


def project_first_kernel(
    tok_ref, cot_ref, down_ref, out_up_ref, weight_ref, total_ref, small_ref, buffer, sems
):
    width = tok_ref.shape[1]
    copies = fetch_columns(weight_ref, buffer, sems, member(0), width)
    small_ref[:, : 3 * RANK] = mm(tok_ref[...], down_ref[...], NT).astype(bf16)
    small_ref[:, 3 * RANK :] = mm(cot_ref[...], out_up_ref[...], NT).astype(bf16)
    for j, copy in enumerate(copies):
        copy.wait()
        for m in range(3):
            total_ref[m, :, j * TILE : (j + 1) * TILE] = mm(tok_ref[...], buffer[j, m])


def project_first(tok, cot, down_t, out_up, weight):
    rows, width = tok.shape
    cols = weight.shape[2]
    tiles = cols // TILE
    return call(
        project_first_kernel,
        [IN_VMEM] * 4 + [IN_HBM],
        [struct((3, rows, cols), f32), struct((rows, 4 * RANK), bf16)],
        6 * rows * width * cols,
        6 * width * cols,
        [pltpu.VMEM((tiles, 3, width, TILE), bf16), pltpu.SemaphoreType.DMA((tiles,))],
    )(tok, cot, down_t, out_up, weight)


def project_next_kernel(one_ref, three_ref, sum_ref, weight_ref, total_ref, buffer, sems):
    width = one_ref.shape[1]
    tiles = weight_ref.shape[2] // TILE
    ones = fetch_columns(weight_ref, buffer, sems, member(-1), width)
    threes = fetch_columns(weight_ref, buffer, sems, member(-3), width, tiles)
    for copies, tok_ref, base, source in (
        (ones, one_ref, 0, sum_ref),
        (threes, three_ref, tiles, total_ref),
    ):
        for j, copy in enumerate(copies):
            at = slice(j * TILE, (j + 1) * TILE)
            copy.wait()
            for m in range(3):
                total_ref[m, :, at] = source[m, :, at] + mm(tok_ref[...], buffer[base + j, m])


def project_next(one, three, total, weight):
    rows, width = one.shape
    cols = weight.shape[2]
    tiles = 2 * (cols // TILE)
    return call(
        project_next_kernel,
        [IN_VMEM] * 3 + [IN_HBM],
        struct((3, rows, cols), f32),
        12 * rows * width * cols,
        12 * width * cols,
        [pltpu.VMEM((tiles, 3, width, TILE), bf16), pltpu.SemaphoreType.DMA((tiles,))],
        {2: 0},
    )(one, three, total, weight)


def split_states(state, mine_ref, given_ref):
    half = mine_ref.shape[0]
    first = first_core()
    for h in range(half):
        low, high = state[h], state[half + h]
        mine_ref[h] = jnp.where(first, low, high)
        given_ref[h] = jnp.where(first, high, low).astype(bf16)


def project_last_kernel(
    tok_ref, sum_ref, small0, small1, small2, small3, up_ref, cot_ref, weight_ref,
    qkv_ref, mine_ref, given_ref, low_ref, cot_out, buffer, state, sems,
):
    width = tok_ref.shape[1]
    copies = fetch_columns(weight_ref, buffer, sems, member(-2), width)
    low = small0[...].astype(f32) + small1[...].astype(f32)
    low = (low + small2[...].astype(f32) + small3[...].astype(f32)).astype(bf16)
    low_ref[...] = low
    cot_out[...] = cot_ref[...]
    for j, copy in enumerate(copies):
        at = slice(j * TILE, (j + 1) * TILE)
        copy.wait()
        for m in range(3):
            total = sum_ref[m, :, at] + mm(tok_ref[...], buffer[j, m])
            total = total + adapter_scale * mm(
                low[:, m * RANK : (m + 1) * RANK], up_ref[m, :, at]
            )
            qkv_ref[m, :, at] = total.astype(bf16)
        for h in range(2 * j, 2 * j + 2):
            head = slice(h * HEAD_DIM, (h + 1) * HEAD_DIM)
            state[h] = mm(qkv_ref[1, :, head], qkv_ref[2, :, head], TN)
    split_states(state, mine_ref, given_ref)


def project_last(tok, total, smalls, up, cot, weight):
    rows, width = tok.shape
    cols = weight.shape[2]
    tiles, heads = cols // TILE, cols // HEAD_DIM
    square = (HEAD_DIM, HEAD_DIM)
    return call(
        project_last_kernel,
        [IN_VMEM] * 8 + [IN_HBM],
        [
            struct((3, rows, cols), bf16),
            struct((heads // 2,) + square, f32),
            struct((heads // 2,) + square, bf16),
            struct((rows, 4 * RANK), bf16),
            struct(cot.shape, bf16),
        ],
        6 * rows * width * cols,
        6 * width * cols,
        [
            pltpu.VMEM((tiles, 3, width, TILE), bf16),
            pltpu.VMEM((heads,) + square, f32),
            pltpu.SemaphoreType.DMA((tiles,)),
        ],
    )(tok, total, *smalls, up, cot, weight)


def attended_gradient_kernel(
    cot0, cot2, cot1, cot3, low_ref, down_ref, weight_ref, out_ref, buffer, sems
):
    width = cot0.shape[1]
    copies = []
    for j in range(weight_ref.shape[0] // TILE):
        copies.append(
            pltpu.make_async_copy(
                weight_ref.at[pl.ds(j * TILE, TILE)], buffer.at[j], sems.at[j]
            )
        )
    for copy in copies:
        copy.start()
    back = low_ref[:, 3 * RANK :]
    for j, copy in enumerate(copies):
        at = slice(j * TILE, (j + 1) * TILE)
        copy.wait()
        total = adapter_scale * mm(back, down_ref[:, at])
        for by, cot_ref in ((0, cot0), (2, cot2), (1, cot1), (3, cot3)):
            chunk = pl.ds(pl.multiple_of(member(-by) * width, width), width)
            total = total + mm(cot_ref[...], buffer[j, :, chunk], NT)
        out_ref[:, at] = total


def attended_gradient(cots, low, down_out, weight):
    rows, width = cots[0].shape
    cols, full = weight.shape
    tiles = cols // TILE
    return call(
        attended_gradient_kernel,
        [IN_VMEM] * 6 + [IN_HBM],
        struct((rows, cols), f32),
        2 * rows * full * cols,
        2 * full * cols,
        [pltpu.VMEM((tiles, TILE, full), bf16), pltpu.SemaphoreType.DMA((tiles,))],
    )(*cots, low, down_out, weight)


def lower_mask(rows):
    s = lax.broadcasted_iota(jnp.int32, (rows, rows), 0)
    t = lax.broadcasted_iota(jnp.int32, (rows, rows), 1)
    return s >= t


def lanes_of(h):
    return slice(h * HEAD_DIM, (h + 1) * HEAD_DIM)


def held_of(own_ref, back_ref, h):
    half = own_ref.shape[0]
    i = h % half
    if h < half:
        return jnp.where(first_core(), own_ref[i], back_ref[i])
    return jnp.where(first_core(), back_ref[i], own_ref[i])


def inside_kernel(qkv_ref, scores_ref, raw_ref):
    mask = lower_mask(raw_ref.shape[0])
    for h in range(scores_ref.shape[0]):
        q, k, v = (qkv_ref[m, :, lanes_of(h)] for m in range(3))
        scores = jnp.where(mask, mm(q, k, NT), 0.0).astype(bf16)
        scores_ref[h] = scores
        raw_ref[:, lanes_of(h)] = mm(scores, v)


def inside_forward(qkv):
    _, rows, cols = qkv.shape
    heads = cols // HEAD_DIM
    return call(
        inside_kernel,
        [IN_VMEM],
        [struct((heads, rows, rows), bf16), struct((rows, cols), f32)],
        4 * rows * cols * rows,
        6 * rows * cols,
    )(qkv)


def forward_kernel(
    qkv_ref, raw_ref, own_ref, back_ref, grad_ref, att_ref, draw_ref, mine_ref, given_ref, state
):
    for h in range(state.shape[0]):
        at = lanes_of(h)
        q = qkv_ref[0, :, at]
        raw = raw_ref[:, at] + mm(q, held_of(own_ref, back_ref, h))
        inverse = lax.rsqrt(jnp.mean(raw * raw, axis=-1, keepdims=True) + epsilon)
        normed = raw * inverse
        att_ref[:, at] = normed.astype(bf16)
        grad = grad_ref[:, at]
        along = jnp.mean(grad * normed, axis=-1, keepdims=True)
        draw = ((grad - normed * along) * inverse).astype(bf16)
        draw_ref[:, at] = draw
        state[h] = mm(q, draw, TN)
    split_states(state, mine_ref, given_ref)


def forward_heads(qkv, raw, held, grad):
    _, rows, cols = qkv.shape
    heads = cols // HEAD_DIM
    square = (HEAD_DIM, HEAD_DIM)
    return call(
        forward_kernel,
        [IN_VMEM] * 5,
        [
            struct((rows, cols), bf16),
            struct((rows, cols), bf16),
            struct((heads // 2,) + square, f32),
            struct((heads // 2,) + square, bf16),
        ],
        8 * rows * cols * HEAD_DIM,
        14 * rows * cols,
        [pltpu.VMEM((heads,) + square, f32)],
    )(qkv, raw, *held, grad)


def to_blocks(out_ref, base, rows):
    for b in range(rows.shape[1] // LANES):
        out_ref[base + b] = rows[:, b * LANES : (b + 1) * LANES]


def within_kernel(
    qkv_ref, scores_ref, own_ref, back_ref, draw_ref, att_ref, low_ref, up_ref,
    dq_ref, dk_ref, dv_ref, back_q_ref, early_ref,
):
    rows = draw_ref.shape[0]
    heads = scores_ref.shape[0]
    mask = lower_mask(rows)
    for h in range(heads):
        at = lanes_of(h)
        q, k, v = (qkv_ref[m, :, at] for m in range(3))
        draw = draw_ref[:, at]
        dscores = jnp.where(mask, mm(draw, v, NT), 0.0).astype(bf16)
        dq = mm(dscores, k) + mm(draw, held_of(own_ref, back_ref, h), NT)
        dq_ref[:, at] = dq.astype(bf16)
        dk_ref[:, at] = mm(dscores, q, TN)
        dv_ref[:, at] = mm(scores_ref[h], draw, TN)
    back_q_ref[...] = mm(dq_ref[...], up_ref[0], NT)
    to_blocks(early_ref, 0, mm(low_ref[:, 3 * RANK :], att_ref[...], TN))
    to_blocks(early_ref, heads, mm(low_ref[:, :RANK], dq_ref[...], TN))


def within_block(qkv, scores, held, draw, att, low, up):
    _, rows, cols = qkv.shape
    heads = cols // HEAD_DIM
    return call(
        within_kernel,
        [IN_VMEM] * 8,
        [
            struct((rows, cols), bf16),
            struct((rows, cols), f32),
            struct((rows, cols), f32),
            struct((rows, RANK), f32),
            struct((2 * heads, RANK, LANES), f32),
        ],
        4 * rows * cols * (4 * rows),
        18 * rows * cols,
    )(qkv, scores, *held, draw, att, low, up)


def across_kernel(
    qkv_ref, own_ref, back_ref, dk_ref, dv_ref, back_q_ref, up_ref, out_ref, low_ref
):
    for h in range(out_ref.shape[2] // HEAD_DIM):
        at = lanes_of(h)
        held = held_of(own_ref, back_ref, h)
        out_ref[0, :, at] = (dk_ref[:, at] + mm(qkv_ref[2, :, at], held, NT)).astype(bf16)
        out_ref[1, :, at] = (dv_ref[:, at] + mm(qkv_ref[1, :, at], held)).astype(bf16)
    low_ref[:, :RANK] = back_q_ref[...].astype(bf16)
    for m in (1, 2):
        low_ref[:, m * RANK : (m + 1) * RANK] = mm(out_ref[m - 1], up_ref[m], NT).astype(bf16)


def across_blocks(qkv, held, dk, dv, back_q, up):
    _, rows, cols = qkv.shape
    return call(
        across_kernel,
        [IN_VMEM] * 7,
        [struct((2, rows, cols), bf16), struct((rows, 3 * RANK), bf16)],
        8 * rows * cols * HEAD_DIM,
        18 * rows * cols,
    )(qkv, *held, dk, dv, back_q, up)


def output_kernel(att_ref, down_ref, weight_ref, own_ref, two_ref, one_ref, three_ref, buffer, sems):
    rows, cols = att_ref.shape
    width = own_ref.shape[1] - LANES
    shifts = (2, 1, 3, 0)
    copies = []
    for i, by in enumerate(shifts):
        chunk = pl.ds(pl.multiple_of(member(by) * width, width), width)
        copies.append(pltpu.make_async_copy(weight_ref.at[:, chunk], buffer.at[i], sems.at[i]))
    for copy in copies:
        copy.start()
    mid = mm(att_ref[...], down_ref[...], NT)
    mid = jnp.concatenate([mid, jnp.zeros((rows, LANES - RANK), f32)], axis=1)
    for i, out_ref in enumerate((two_ref, one_ref, three_ref, own_ref)):
        copies[i].wait()
        for j in range(width // TILE):
            at = slice(j * TILE, (j + 1) * TILE)
            out_ref[:, at] = mm(att_ref[...], buffer[i, :, at]).astype(out_ref.dtype)
        out_ref[:, width:] = mid.astype(out_ref.dtype)


def output_parts(att, down_out, weight, width):
    rows, cols = att.shape
    wide = width + LANES
    return call(
        output_kernel,
        [IN_VMEM] * 2 + [IN_HBM],
        [struct((rows, wide), f32)] + [struct((rows, wide), bf16)] * 3,
        8 * rows * cols * width,
        8 * cols * width,
        [pltpu.VMEM((4, cols, width), bf16), pltpu.SemaphoreType.DMA((4,))],
    )(att, down_out, weight)


def output_sum_kernel(own_ref, two_ref, one_ref, three_ref, up_ref, cot_ref, out_ref, grad_ref):
    width = out_ref.shape[1]
    parts = [two_ref, one_ref, three_ref]
    mid = own_ref[:, width:]
    for part in parts:
        mid = mid + part[:, width:].astype(f32)
    mid = mid[:, :RANK].astype(bf16)
    total = own_ref[:, :width] + adapter_scale * mm(mid, up_ref[...])
    for part in parts:
        total = total + part[:, :width].astype(f32)
    out_ref[...] = total.astype(bf16)
    to_blocks(grad_ref, 0, mm(mid, cot_ref[...], TN))


def output_sum(own, parts, up, cot):
    rows, width = cot.shape
    return call(
        output_sum_kernel,
        [IN_VMEM] * 6,
        [struct((rows, width), bf16), struct((width // LANES, RANK, LANES), f32)],
        8 * rows * width * RANK,
        14 * rows * width,
    )(own, *parts, up, cot)


def query_kernel(dq_ref, weight_ref, out_ref, buffer, sems):
    parts, _, width = out_ref.shape
    copies = []
    for p in range(parts):
        copies.append(
            pltpu.make_async_copy(
                weight_ref.at[0, pl.ds(p * width, width)], buffer.at[p], sems.at[p]
            )
        )
    for copy in copies:
        copy.start()
    for p, copy in enumerate(copies):
        copy.wait()
        out_ref[p] = mm(dq_ref[...], buffer[p], NT)


def query_part(dq, weight, width):
    rows, cols = dq.shape
    parts = weight.shape[1] // width
    return call(
        query_kernel,
        [IN_VMEM, IN_HBM],
        struct((parts, rows, width), f32),
        2 * rows * cols * width * parts,
        2 * cols * width * parts,
        [pltpu.VMEM((parts, width, cols), bf16), pltpu.SemaphoreType.DMA((parts,))],
    )(dq, weight)


def input_kernel(by, dkv_ref, dq_ref, weight_ref, out_ref, buffer, sems):
    width = out_ref.shape[1]
    part = member(by)
    base = pl.multiple_of(part * width, width)
    copies = []
    for m in range(2):
        copies.append(
            pltpu.make_async_copy(
                weight_ref.at[m + 1, pl.ds(base, width)], buffer.at[m], sems.at[m]
            )
        )
    for copy in copies:
        copy.start()
    copies[0].wait()
    total = dq_ref[part] + mm(dkv_ref[0], buffer[0], NT)
    copies[1].wait()
    out_ref[...] = (total + mm(dkv_ref[1], buffer[1], NT)).astype(out_ref.dtype)


def input_part(by, dkv, dq_parts, weight, width, dtype):
    _, rows, cols = dkv.shape
    return call(
        functools.partial(input_kernel, by),
        [IN_VMEM] * 2 + [IN_HBM],
        struct((rows, width), dtype),
        4 * rows * cols * width,
        4 * cols * width,
        [pltpu.VMEM((2, width, cols), bf16), pltpu.SemaphoreType.DMA((2,))],
    )(dkv, dq_parts, weight)


def input_sum_kernel(own_ref, two_ref, one_ref, three_ref, low_ref, down_ref, out_ref):
    total = own_ref[...] + adapter_scale * mm(low_ref[...], down_ref[...])
    for part in (two_ref, one_ref, three_ref):
        total = total + part[...].astype(f32)
    out_ref[...] = total.astype(bf16)


def input_sum(own, parts, low, down_t):
    rows, width = own.shape
    return call(
        input_sum_kernel,
        [IN_VMEM] * 6,
        struct((rows, width), bf16),
        6 * rows * width * RANK,
        12 * rows * width,
    )(own, *parts, low, down_t)


def grads_kernel(
    back0, back2, back1, back3, tok_ref, low_ref, dkv_ref, early_ref, up_out_ref,
    *refs,
):
    back_ref, mine_ref, given_ref, packed = refs[-4:]
    back = back0[...].astype(f32) + back2[...].astype(f32)
    back = (back + back1[...].astype(f32) + back3[...].astype(f32)).astype(bf16)
    back_ref[...] = back
    down = mm(back, tok_ref[...], TN)
    at = 0
    for m in range(3):
        to_blocks(packed, at, down[m * RANK : (m + 1) * RANK])
        at += tok_ref.shape[1] // LANES
    for ref in (up_out_ref, early_ref):
        packed[at : at + ref.shape[0]] = ref[...]
        at += ref.shape[0]
    for m in (1, 2):
        to_blocks(packed, at, mm(low_ref[:, m * RANK : (m + 1) * RANK], dkv_ref[m - 1], TN))
        at += dkv_ref.shape[2] // LANES
    half = mine_ref.shape[0]
    first = first_core()
    mine_ref[...] = jnp.where(first, packed[:half], packed[half:])
    given_ref[...] = jnp.where(first, packed[half:], packed[:half]).astype(bf16)


def grads(backs, tokens, low, dkv, early, up_out, unread):
    rows, width = tokens.shape
    cols = dkv.shape[2]
    half = 2 * (width + cols) // LANES
    return call(
        grads_kernel,
        [IN_VMEM] * 9 + [UNREAD] * len(unread),
        [
            struct(backs[0].shape, bf16),
            struct((half, RANK, LANES), f32),
            struct((half, RANK, LANES), bf16),
        ],
        2 * rows * RANK * (3 * width + 2 * cols),
        2 * dkv.size + 2 * tokens.size,
        [pltpu.VMEM((2 * half, RANK, LANES), f32)],
    )(*backs, tokens, low, dkv, early, up_out, *unread)


def unpack_kernel(scale, own_ref, back_ref, down_ref, up_ref, down_out_ref, up_out_ref):
    half = own_ref.shape[0]
    at = 0

    def take(count):
        nonlocal at
        at += count
        first = first_core()
        blocks = []
        for b in range(at - count, at):
            own, back = own_ref[b % half], back_ref[b % half]
            block = jnp.where(first, own, back) if b < half else jnp.where(first, back, own)
            blocks.append(block.astype(f32))
        return scale * jnp.concatenate(blocks, axis=1)

    wide, heads = up_out_ref.shape[1] // LANES, down_out_ref.shape[1] // LANES
    for m in range(3):
        down_ref[m] = take(wide)
    up_out_ref[...] = take(wide)
    down_out_ref[...] = take(heads)
    for m in range(3):
        up_ref[m] = take(heads)


def unpack(own, back, scale, width, cols):
    return call(
        functools.partial(unpack_kernel, scale),
        [IN_VMEM] * 2,
        [
            struct((3, RANK, width), f32),
            struct((3, RANK, cols), f32),
            struct((RANK, cols), f32),
            struct((RANK, width), f32),
        ],
        own.size,
        12 * own.size,
    )(own, back)


def shift(array, by):
    n = lax.axis_size("head")
    return lax.ppermute(array, "head", [(i, (i + by) % n) for i in range(n)])


def from_head(array):
    return [shift(array, by) for by in (2, 1, 3)]


def swap_cores(array):
    n = lax.axis_size("ctx")
    return lax.ppermute(array, "ctx", [(i, i ^ 1) for i in range(n)])


def chip_place():
    n = lax.axis_size("ctx")
    chip = lax.axis_index("ctx") // 2
    side = {32: 4}[n]
    return lax.rem(chip, side), chip // side


def along(array, axis, by):
    n = lax.axis_size("ctx")
    side = {32: 4}[n]
    pairs = []
    for i in range(n):
        core, x, z = i % 2, (i // 2) % side, i // (2 * side)
        if axis == "x":
            x = (x + by) % side
        else:
            z = (z + by) % side
        pairs.append((i, (z * side + x) * 2 + core))
    return lax.ppermute(array, "ctx", pairs)


def three(array, axis):
    return [along(array, axis, by) for by in (1, 3, 2)]


def pair_kernel(mine_ref, got_ref, out_ref):
    out_ref[...] = (mine_ref[...] + got_ref[...].astype(f32)).astype(bf16)


def before_sum(reverse, place, refs):
    total = jnp.zeros(refs[0].shape, f32)
    for by, ref in zip((1, 3, 2), refs):
        wanted = (place < by) if reverse else (place >= by)
        total = total + jnp.where(wanted, ref[...].astype(f32), 0.0)
    return total


def row_kernel(reverse, mine_ref, got_ref, one_ref, three_ref, two_ref, *refs):
    row_ref, before_ref = refs[-2:]
    others = (one_ref, three_ref, two_ref)
    total = mine_ref[...] + got_ref[...].astype(f32)
    for ref in others:
        total = total + ref[...].astype(f32)
    row_ref[...] = total.astype(bf16)
    before_ref[...] = before_sum(reverse, chip_place()[0], others)


def combine_kernel(
    reverse, mine_ref, got_ref, before_ref, one_ref, three_ref, two_ref, *refs
):
    own_ref, other_ref = refs[-2:]
    chip = before_ref[...] + before_sum(reverse, chip_place()[1], (one_ref, three_ref, two_ref))
    first = first_core() != reverse
    own_ref[...] = jnp.where(first, chip, chip + got_ref[...].astype(f32)).astype(bf16)
    other_ref[...] = jnp.where(first, chip + mine_ref[...], chip).astype(bf16)


def glue(kernel, operands, out_dtypes, unread=()):
    shape = operands[0].shape
    return call(
        kernel,
        [IN_VMEM] * len(operands) + [UNREAD] * len(unread),
        [struct(shape, dtype) for dtype in out_dtypes],
        operands[0].size,
        8 * operands[0].size,
    )(*operands, *unread)


def scan_states(mine, given, reverse, during_first, during_second):
    got = swap_cores(given)
    (pair,) = glue(pair_kernel, [mine, got], [bf16])
    row, before = glue(
        functools.partial(row_kernel, reverse),
        [mine, got] + three(pair, "x"),
        [bf16, f32],
        during_first,
    )
    own, other = glue(
        functools.partial(combine_kernel, reverse),
        [mine, got, before] + three(row, "z"),
        [bf16, bf16],
        during_second,
    )
    return own, swap_cores(other)


def row_sum_kernel(count, mine_ref, *refs):
    total = mine_ref[...].astype(f32)
    for ref in refs[:count]:
        total = total + ref[...].astype(f32)
    refs[-1][...] = total.astype(bf16)


def sum_over_ctx(mine, given, during_first, during_second):
    got = swap_cores(given)
    (pair,) = glue(functools.partial(row_sum_kernel, 1), [mine, got], [bf16])
    (row,) = glue(
        functools.partial(row_sum_kernel, 4),
        [mine, got] + three(pair, "x"),
        [bf16],
        during_first,
    )
    (total,) = glue(
        functools.partial(row_sum_kernel, 3), [row] + three(row, "z"), [bf16], during_second
    )
    return total, swap_cores(total)


def on_device(
    tokens,
    query_key_value_weight,
    output_weight,
    input_down_weights,
    input_up_weights,
    output_down_weight,
    output_up_weight,
    cotangent,
):
    rows, width = tokens.shape
    cols = query_key_value_weight.shape[2]
    n = lax.axis_size("ctx")
    scale_factor = adapter_scale * (rows * n) ** (-0.5)
    down_t = input_down_weights.transpose(0, 2, 1).reshape(3 * RANK, width)
    down_out_t = output_down_weight.T

    two, one, three = from_head(tokens)
    total, small = project_first(
        tokens, cotangent, down_t, output_up_weight, query_key_value_weight
    )
    smalls = [small] + from_head(small)
    total = project_next(one, three, total, query_key_value_weight)
    qkv, mine, given, low, cot_late = project_last(
        two, total, smalls, input_up_weights, cotangent, query_key_value_weight
    )

    cots = [cotangent] + from_head(cot_late)
    scores, raw = inside_forward(qkv)
    grad = attended_gradient(cots, low, down_out_t, output_weight)
    held = scan_states(mine, given, False, [raw], [grad])

    attended, d_raw, mine, given = forward_heads(qkv, raw, held, grad)
    out_own, *out_sent = output_parts(attended, down_out_t, output_weight, width)
    out_got = [shift(part, by) for part, by in zip(out_sent, (2, 1, 3))]
    dq, dk_within, dv_within, back_q, early = within_block(
        qkv, scores, held, d_raw, attended, low, input_up_weights
    )
    dq_parts = query_part(dq, query_key_value_weight, width)
    suffix = scan_states(mine, given, True, [out_own], [early, dq_parts])

    dkv, back_part = across_blocks(qkv, suffix, dk_within, dv_within, back_q, input_up_weights)
    backs = [back_part] + from_head(back_part)
    grad_sent = [
        input_part(by, dkv, dq_parts, query_key_value_weight, width, bf16) for by in (2, 1, 3)
    ]
    grad_got = [shift(part, by) for part, by in zip(grad_sent, (2, 1, 3))]
    grad_own = input_part(0, dkv, dq_parts, query_key_value_weight, width, f32)

    output, grad_up_out = output_sum(out_own, out_got, output_up_weight, cotangent)
    back_low, mine, given = grads(
        backs, tokens, low, dkv, early, grad_up_out, grad_sent[:2]
    )
    sums = sum_over_ctx(mine, given, [grad_sent[2]], [grad_own])
    input_grad = input_sum(grad_own, grad_got, back_low, down_t)
    grad_down_qkv, grad_up_qkv, grad_down_out, grad_up_out = unpack(
        *sums, scale_factor, width, cols
    )
    return (
        output,
        input_grad,
        grad_down_qkv.transpose(0, 2, 1),
        grad_up_qkv,
        grad_down_out.T,
        grad_up_out,
    )


def solution(mesh):
    return jax.shard_map(
        on_device,
        mesh=mesh,
        in_specs=(
            P("ctx", "head"),
            P(None, None, "head"),
            P("head", None),
            P(None, "head", None),
            P(None, None, "head"),
            P("head", None),
            P(None, "head"),
            P("ctx", "head"),
        ),
        out_specs=(
            P("ctx", "head"),
            P("ctx", "head"),
            P(None, "head", None),
            P(None, None, "head"),
            P("head", None),
            P(None, "head"),
        ),
        check_vma=False,
    )
```

```python
import functools

import jax
import jax.numpy as jnp
from jax import lax
from jax.experimental import pallas as pl
from jax.experimental.pallas import tpu as pltpu
from jax.sharding import PartitionSpec as P

HEAD_DIM = 128
RANK = 16
TILE = 256
LANES = 128
adapter_scale = 0.5
epsilon = 1e-06
bf16 = jnp.bfloat16
f32 = jnp.float32
HINT = 2 * 10**10
VMEM_BYTES = 12 * 2**20

NN = (((1,), (0,)), ((), ()))
NT = (((1,), (1,)), ((), ()))
TN = (((0,), (0,)), ((), ()))

IN_HBM = pl.BlockSpec(memory_space=pltpu.HBM)
IN_VMEM = pl.BlockSpec(memory_space=pltpu.VMEM)
UNREAD = pl.BlockSpec(memory_space=pl.ANY)


def mm(a, b, dims=NN):
    return lax.dot_general(a, b, dims, preferred_element_type=f32)


def struct(shape, dtype):
    return jax.ShapeDtypeStruct(shape, dtype)


def call(kernel, specs, out_shape, flops, moved, scratch=(), aliases=None):
    many = isinstance(out_shape, (list, tuple))
    return pl.pallas_call(
        kernel,
        in_specs=specs,
        out_specs=[IN_VMEM] * len(out_shape) if many else IN_VMEM,
        out_shape=out_shape,
        scratch_shapes=list(scratch),
        input_output_aliases=aliases or {},
        compiler_params=pltpu.CompilerParams(vmem_limit_bytes=VMEM_BYTES),
        cost_estimate=pl.CostEstimate(flops=flops, bytes_accessed=moved, transcendentals=0),
    )


def member(shift):
    return lax.rem(lax.axis_index("head") + shift + 4, 4)


def first_core():
    return lax.rem(lax.axis_index("ctx"), 2) == 0


def chunk_rows(weight_ref, m, shift, width):
    return weight_ref[m, pl.ds(pl.multiple_of(member(shift) * width, width), width)]


def start_kernel(tok_ref, down_ref, top_ref, bottom_ref):
    half = top_ref.shape[0]
    width = tok_ref.shape[1]
    top_ref[:, :width] = tok_ref[:half]
    bottom_ref[:, :width] = tok_ref[half:]
    small = mm(tok_ref[...], down_ref[...], NT)
    value = small.astype(bf16)
    rest = (small - value.astype(f32)).astype(bf16)
    pad = jnp.zeros((half, LANES - 6 * RANK), bf16)
    small = jnp.concatenate(
        [value[:half], rest[:half], pad, value[half:], rest[half:], pad], axis=1
    )
    top_ref[:, width:] = small
    bottom_ref[:, width:] = small


def start(tok, down_t):
    rows, width = tok.shape
    return call(
        start_kernel,
        [IN_VMEM] * 2,
        [struct((rows // 2, width + 2 * LANES), bf16)] * 2,
        HINT,
        6 * rows * width,
    )(tok, down_t)


def project_first_kernel(tok_ref, weight_ref, total_ref):
    for m in range(3):
        total_ref[m] = mm(tok_ref[...], chunk_rows(weight_ref, m, 0, tok_ref.shape[1]))


def project_first(tok, weight):
    rows, width = tok.shape
    cols = weight.shape[2]
    return call(
        project_first_kernel,
        [IN_VMEM] * 2,
        struct((3, rows, cols), f32),
        6 * rows * width * cols,
        6 * width * cols,
    )(tok, weight)


def joined(buffer, top_ref, bottom_ref):
    half = top_ref.shape[0]
    buffer[:half] = top_ref[:, : buffer.shape[1]]
    buffer[half:] = bottom_ref[:, : buffer.shape[1]]
    return buffer[...]


def project_next_kernel(by, top_ref, bottom_ref, sum_ref, weight_ref, total_ref, buffer):
    tok = joined(buffer, top_ref, bottom_ref)
    for m in range(3):
        total_ref[m] = sum_ref[m] + mm(tok, chunk_rows(weight_ref, m, -by, tok.shape[1]))


def project_next(by, halves, total, weight, width):
    _, rows, cols = total.shape
    return call(
        functools.partial(project_next_kernel, by),
        [IN_VMEM] * 4,
        struct((3, rows, cols), f32),
        6 * rows * width * cols,
        6 * width * cols,
        [pltpu.VMEM((rows, width), bf16)],
        {2: 0},
    )(*halves, total, weight)


def cotangent_kernel(cot_ref, out_up_ref, unread, out_ref):
    rows, width = cot_ref.shape
    out_ref[:, :width] = cot_ref[...]
    back = mm(cot_ref[...], out_up_ref[...], NT).astype(bf16)
    out_ref[:, width:] = jnp.concatenate(
        [back, jnp.zeros((rows, LANES - RANK), bf16)], axis=1
    )


def cotangent_parts(cot, out_up, unread):
    rows, width = cot.shape
    return call(
        cotangent_kernel,
        [IN_VMEM] * 2 + [UNREAD],
        struct((rows, width + LANES), bf16),
        2 * rows * width * RANK,
        4 * rows * width,
    )(cot, out_up, unread)


def split_states(state, mine_ref, given_ref):
    half = mine_ref.shape[0]
    first = first_core()
    for h in range(half):
        low, high = state[h], state[half + h]
        mine_ref[h] = jnp.where(first, low, high)
        given_ref[h] = jnp.where(first, high, low).astype(bf16)


def project_last_kernel(
    top_ref, bottom_ref, sum_ref, own_ref, one_ref, three_ref, up_ref, weight_ref,
    qkv_ref, mine_ref, given_ref, low_ref, state, buffer,
):
    tok = joined(buffer, top_ref, bottom_ref)
    half = top_ref.shape[0]
    width = tok.shape[1]
    low = sum(
        ref[:, width:].astype(f32) for ref in (own_ref, one_ref, three_ref, top_ref)
    )
    for at, part in ((slice(0, half), low[:, :LANES]), (slice(half, 2 * half), low[:, LANES:])):
        low_ref[at] = (part[:, : 3 * RANK] + part[:, 3 * RANK : 6 * RANK]).astype(bf16)
    for m in (1, 2, 0):
        total = sum_ref[m] + mm(tok, chunk_rows(weight_ref, m, -2, width))
        total = total + adapter_scale * mm(low_ref[:, m * RANK : (m + 1) * RANK], up_ref[m])
        qkv_ref[m] = total.astype(bf16)
    for h in range(state.shape[0]):
        at = slice(h * HEAD_DIM, (h + 1) * HEAD_DIM)
        state[h] = mm(qkv_ref[1, :, at], qkv_ref[2, :, at], TN)
    split_states(state, mine_ref, given_ref)


def project_last(halves, total, smalls, up, weight, width):
    _, rows, cols = total.shape
    heads = cols // HEAD_DIM
    square = (HEAD_DIM, HEAD_DIM)
    return call(
        project_last_kernel,
        [IN_VMEM] * 8,
        [
            struct((3, rows, cols), bf16),
            struct((heads // 2,) + square, f32),
            struct((heads // 2,) + square, bf16),
            struct((rows, 3 * RANK), bf16),
        ],
        6 * rows * width * cols,
        6 * width * cols,
        [pltpu.VMEM((heads,) + square, f32), pltpu.VMEM((rows, width), bf16)],
    )(*halves, total, *smalls, up, weight)


def attended_gradient_kernel(
    cot0, cot1, cot3, top_ref, bottom_ref, down_ref, weight_ref, out_ref, back_ref, buffer
):
    width = cot0.shape[1] - LANES
    joined(buffer, top_ref, bottom_ref)
    refs = ((0, cot0), (1, cot1), (3, cot3), (2, buffer))
    back = sum(ref[:, width:].astype(f32) for _, ref in refs).astype(bf16)[:, :RANK]
    back_ref[...] = back
    total = adapter_scale * mm(back, down_ref[...])
    for by, ref in refs:
        chunk = pl.ds(pl.multiple_of(member(-by) * width, width), width)
        total = total + mm(ref[:, :width], weight_ref[:, chunk], NT)
    out_ref[...] = total


def attended_gradient(cots, down_out, weight):
    rows, wide = cots[0].shape
    cols, full = weight.shape
    return call(
        attended_gradient_kernel,
        [IN_VMEM] * 7,
        [struct((rows, cols), f32), struct((rows, RANK), bf16)],
        2 * rows * full * cols,
        2 * full * cols,
        [pltpu.VMEM((rows, wide), bf16)],
    )(*cots, down_out, weight)


def lower_mask(rows):
    s = lax.broadcasted_iota(jnp.int32, (rows, rows), 0)
    t = lax.broadcasted_iota(jnp.int32, (rows, rows), 1)
    return s >= t


def lanes_of(h):
    return slice(h * HEAD_DIM, (h + 1) * HEAD_DIM)


def held_of(own_ref, back_ref, h):
    half = own_ref.shape[0]
    i = h % half
    if h < half:
        return jnp.where(first_core(), own_ref[i], back_ref[i])
    return jnp.where(first_core(), back_ref[i], own_ref[i])


def inside_kernel(qkv_ref, unread, scores_ref, raw_ref):
    mask = lower_mask(raw_ref.shape[0])
    for h in range(scores_ref.shape[0]):
        q, k, v = (qkv_ref[m, :, lanes_of(h)] for m in range(3))
        scores = jnp.where(mask, mm(q, k, NT), 0.0).astype(bf16)
        scores_ref[h] = scores
        raw_ref[:, lanes_of(h)] = mm(scores, v)


def inside_forward(qkv, unread):
    _, rows, cols = qkv.shape
    heads = cols // HEAD_DIM
    return call(
        inside_kernel,
        [IN_VMEM, UNREAD],
        [struct((heads, rows, rows), bf16), struct((rows, cols), f32)],
        4 * rows * cols * rows,
        6 * rows * cols,
    )(qkv, unread)


def halves_kernel(one_ref, three_ref, unread, top_ref, bottom_ref):
    half = top_ref.shape[0]
    top_ref[...] = one_ref[:half]
    bottom_ref[...] = three_ref[half:]


def halves(one, three, unread):
    rows, width = one.shape
    return call(
        halves_kernel,
        [IN_VMEM] * 2 + [UNREAD],
        [struct((rows // 2, width), bf16)] * 2,
        rows * width,
        4 * rows * width,
    )(one, three, unread)


def forward_kernel(
    qkv_ref, raw_ref, own_ref, back_ref, grad_ref, att_ref, draw_ref, mine_ref, given_ref, state
):
    for h in range(state.shape[0]):
        at = lanes_of(h)
        q = qkv_ref[0, :, at]
        raw = raw_ref[:, at] + mm(q, held_of(own_ref, back_ref, h))
        inverse = lax.rsqrt(jnp.mean(raw * raw, axis=-1, keepdims=True) + epsilon)
        normed = raw * inverse
        att_ref[:, at] = normed.astype(bf16)
        grad = grad_ref[:, at]
        along = jnp.mean(grad * normed, axis=-1, keepdims=True)
        draw = ((grad - normed * along) * inverse).astype(bf16)
        draw_ref[:, at] = draw
        state[h] = mm(q, draw, TN)
    split_states(state, mine_ref, given_ref)


def forward_heads(qkv, raw, held, grad):
    _, rows, cols = qkv.shape
    heads = cols // HEAD_DIM
    square = (HEAD_DIM, HEAD_DIM)
    return call(
        forward_kernel,
        [IN_VMEM] * 5,
        [
            struct((rows, cols), bf16),
            struct((rows, cols), bf16),
            struct((heads // 2,) + square, f32),
            struct((heads // 2,) + square, bf16),
        ],
        8 * rows * cols * HEAD_DIM,
        14 * rows * cols,
        [pltpu.VMEM((heads,) + square, f32)],
    )(qkv, raw, *held, grad)


def to_blocks(out_ref, base, rows):
    for b in range(rows.shape[1] // LANES):
        out_ref[base + b] = rows[:, b * LANES : (b + 1) * LANES]


def within_kernel(
    qkv_ref, scores_ref, own_ref, back_ref, draw_ref, att_ref, back_mid_ref, low_ref, up_ref,
    down_ref, unread, dq_ref, dk_ref, dv_ref, back_q_ref, mid_ref, early_ref,
):
    rows = draw_ref.shape[0]
    heads = scores_ref.shape[0]
    mask = lower_mask(rows)
    for h in range(heads):
        at = lanes_of(h)
        q, k, v = (qkv_ref[m, :, at] for m in range(3))
        draw = draw_ref[:, at]
        dscores = jnp.where(mask, mm(draw, v, NT), 0.0).astype(bf16)
        dq = mm(dscores, k) + mm(draw, held_of(own_ref, back_ref, h), NT)
        dq_ref[:, at] = dq.astype(bf16)
        dk_ref[:, at] = mm(dscores, q, TN)
        dv_ref[:, at] = mm(scores_ref[h], draw, TN)
    back_q_ref[...] = mm(dq_ref[...], up_ref[0], NT)
    mid_ref[...] = mm(att_ref[...], down_ref[...], NT)
    to_blocks(early_ref, 0, mm(back_mid_ref[...], att_ref[...], TN))
    to_blocks(early_ref, heads, mm(low_ref[:, :RANK], dq_ref[...], TN))


def within_block(qkv, scores, held, draw, att, back_mid, low, up, down_out, unread):
    _, rows, cols = qkv.shape
    heads = cols // HEAD_DIM
    return call(
        within_kernel,
        [IN_VMEM] * 10 + [UNREAD],
        [
            struct((rows, cols), bf16),
            struct((rows, cols), f32),
            struct((rows, cols), f32),
            struct((rows, RANK), f32),
            struct((rows, RANK), f32),
            struct((2 * heads, RANK, LANES), f32),
        ],
        4 * rows * cols * (4 * rows),
        18 * rows * cols,
    )(qkv, scores, *held, draw, att, back_mid, low, up, down_out, unread)


def across_kernel(
    qkv_ref, own_ref, back_ref, dk_ref, dv_ref, back_q_ref, mid_ref, up_ref, out_ref, low_ref
):
    for h in range(out_ref.shape[2] // HEAD_DIM):
        at = lanes_of(h)
        held = held_of(own_ref, back_ref, h)
        out_ref[0, :, at] = (dk_ref[:, at] + mm(qkv_ref[2, :, at], held, NT)).astype(bf16)
        out_ref[1, :, at] = (dv_ref[:, at] + mm(qkv_ref[1, :, at], held)).astype(bf16)
    low_ref[:, :RANK] = back_q_ref[...].astype(bf16)
    low_ref[:, 3 * RANK :] = mid_ref[...].astype(bf16)
    for m in (1, 2):
        low_ref[:, m * RANK : (m + 1) * RANK] = mm(out_ref[m - 1], up_ref[m], NT).astype(bf16)


def across_blocks(qkv, held, dk, dv, back_q, mid, up):
    _, rows, cols = qkv.shape
    return call(
        across_kernel,
        [IN_VMEM] * 8,
        [struct((2, rows, cols), bf16), struct((rows, 4 * RANK), bf16)],
        8 * rows * cols * HEAD_DIM,
        18 * rows * cols,
    )(qkv, *held, dk, dv, back_q, mid, up)


def output_product(by, att_ref, weight_ref, width):
    chunk = pl.ds(pl.multiple_of(member(by) * width, width), width)
    return mm(att_ref[...], weight_ref[:, chunk])


def output_far_kernel(att_ref, weight_ref, unread0, unread1, top_ref, bottom_ref):
    half, width = top_ref.shape
    part = output_product(2, att_ref, weight_ref, width).astype(bf16)
    top_ref[...] = part[:half]
    bottom_ref[...] = part[half:]


def output_far(att, weight, width, unread):
    rows, cols = att.shape
    return call(
        output_far_kernel,
        [IN_VMEM] * 2 + [UNREAD] * 2,
        [struct((rows // 2, width), bf16)] * 2,
        2 * rows * cols * width,
        2 * cols * width,
    )(att, weight, *unread)


def output_near_kernel(
    att_ref, relay_top, relay_bottom, weight_ref, unread, own_ref, one_ref, three_ref
):
    half, width = relay_top.shape
    own_ref[...] = output_product(0, att_ref, weight_ref, width)
    one = output_product(1, att_ref, weight_ref, width)
    one_ref[:half] = (one[:half] + relay_top[...].astype(f32)).astype(bf16)
    one_ref[half:] = one[half:].astype(bf16)
    three = output_product(3, att_ref, weight_ref, width)
    three_ref[:half] = three[:half].astype(bf16)
    three_ref[half:] = (three[half:] + relay_bottom[...].astype(f32)).astype(bf16)


def output_near(att, relays, weight, unread):
    rows, cols = att.shape
    width = relays[0].shape[1]
    return call(
        output_near_kernel,
        [IN_VMEM] * 4 + [UNREAD],
        [struct((rows, width), f32)] + [struct((rows, width), bf16)] * 2,
        6 * rows * cols * width,
        6 * cols * width,
    )(att, *relays, weight, unread)


def output_sum_kernel(own_ref, one_ref, three_ref, low_ref, up_ref, unread, out_ref):
    total = own_ref[...] + one_ref[...].astype(f32) + three_ref[...].astype(f32)
    total = total + adapter_scale * mm(low_ref[:, 3 * RANK :], up_ref[...])
    out_ref[...] = total.astype(bf16)


def output_sum(own, parts, low, up, unread):
    rows, width = own.shape
    return call(
        output_sum_kernel,
        [IN_VMEM] * 5 + [UNREAD],
        struct((rows, width), bf16),
        2 * rows * width * RANK,
        10 * rows * width,
    )(own, *parts, low, up, unread)


def query_kernel(dq_ref, weight_ref, unread, out_ref):
    parts, _, width = out_ref.shape
    for p in range(parts):
        out_ref[p] = mm(dq_ref[...], weight_ref[0, p * width : (p + 1) * width], NT)


def query_part(dq, weight, width, unread):
    rows, cols = dq.shape
    parts = weight.shape[1] // width
    return call(
        query_kernel,
        [IN_VMEM] * 2 + [UNREAD],
        struct((parts, rows, width), f32),
        2 * rows * cols * width * parts,
        2 * cols * width * parts,
    )(dq, weight, unread)


def input_product(by, dkv_ref, dq_ref, weight_ref):
    total = dq_ref[member(by)]
    for m in range(2):
        total = total + mm(
            dkv_ref[m], chunk_rows(weight_ref, m + 1, by, total.shape[1]), NT
        )
    return total


def input_piece_kernel(by, dkv_ref, dq_ref, weight_ref, unread, out_ref):
    out_ref[...] = input_product(by, dkv_ref, dq_ref, weight_ref).astype(bf16)


def input_own_kernel(dkv_ref, dq_ref, weight_ref, unread, out_ref):
    out_ref[...] = input_product(0, dkv_ref, dq_ref, weight_ref)


def input_call(kernel, dkv, dq_parts, weight, out, *more):
    _, rows, cols = dkv.shape
    width = dq_parts.shape[2]
    return call(
        kernel,
        [IN_VMEM] * 3 + [UNREAD] * len(more),
        out,
        4 * rows * cols * width,
        4 * cols * width,
    )(dkv, dq_parts, weight, *more)


def input_sum_kernel(own_ref, two_ref, one_ref, three_ref, low_ref, down_ref, out_ref):
    total = own_ref[...] + adapter_scale * mm(low_ref[:, : 3 * RANK], down_ref[...])
    for ref in (two_ref, one_ref, three_ref):
        total = total + ref[...].astype(f32)
    out_ref[...] = total.astype(bf16)


def input_sum(own, parts, low, down_t):
    rows, width = own.shape
    return call(
        input_sum_kernel,
        [IN_VMEM] * 6,
        struct((rows, width), bf16),
        6 * rows * width * RANK,
        12 * rows * width,
    )(own, *parts, low, down_t)


def grads_kernel(
    back0, back2, back1, back3, tok_ref, cot_ref, low_ref, dkv_ref, early_ref,
    *refs,
):
    back_ref, mine_ref, given_ref, packed = refs[-4:]
    back = back0[...].astype(f32) + back2[...].astype(f32)
    back = (back + back1[...].astype(f32) + back3[...].astype(f32)).astype(bf16)
    back_ref[...] = back
    down = mm(back[:, : 3 * RANK], tok_ref[...], TN)
    up_out = mm(back[:, 3 * RANK :], cot_ref[...], TN)
    at = 0
    for m in range(3):
        to_blocks(packed, at, down[m * RANK : (m + 1) * RANK])
        at += tok_ref.shape[1] // LANES
    to_blocks(packed, at, up_out)
    at += cot_ref.shape[1] // LANES
    packed[at : at + early_ref.shape[0]] = early_ref[...]
    at += early_ref.shape[0]
    for m in (1, 2):
        to_blocks(packed, at, mm(low_ref[:, m * RANK : (m + 1) * RANK], dkv_ref[m - 1], TN))
        at += dkv_ref.shape[2] // LANES
    half = mine_ref.shape[0]
    first = first_core()
    mine_ref[...] = jnp.where(first, packed[:half], packed[half:])
    given_ref[...] = jnp.where(first, packed[half:], packed[:half]).astype(bf16)


def grads(backs, tokens, cot, low, dkv, early, unread):
    rows, width = tokens.shape
    cols = dkv.shape[2]
    half = 2 * (width + cols) // LANES
    return call(
        grads_kernel,
        [IN_VMEM] * 9 + [UNREAD] * len(unread),
        [
            struct(backs[0].shape, bf16),
            struct((half, RANK, LANES), f32),
            struct((half, RANK, LANES), bf16),
        ],
        2 * rows * RANK * (3 * width + 2 * cols),
        2 * dkv.size + 2 * tokens.size,
        [pltpu.VMEM((2 * half, RANK, LANES), f32)],
    )(*backs, tokens, cot, low, dkv, early, *unread)


def unpack_kernel(scale, own_ref, back_ref, down_ref, up_ref, down_out_ref, up_out_ref):
    half = own_ref.shape[0]
    at = 0

    def take(count):
        nonlocal at
        at += count
        first = first_core()
        blocks = []
        for b in range(at - count, at):
            own, back = own_ref[b % half], back_ref[b % half]
            block = jnp.where(first, own, back) if b < half else jnp.where(first, back, own)
            blocks.append(block.astype(f32))
        return scale * jnp.concatenate(blocks, axis=1)

    wide, heads = up_out_ref.shape[1] // LANES, down_out_ref.shape[1] // LANES
    for m in range(3):
        down_ref[m] = take(wide)
    up_out_ref[...] = take(wide)
    down_out_ref[...] = take(heads)
    for m in range(3):
        up_ref[m] = take(heads)


def unpack(own, back, scale, width, cols):
    return call(
        functools.partial(unpack_kernel, scale),
        [IN_VMEM] * 2,
        [
            struct((3, RANK, width), f32),
            struct((3, RANK, cols), f32),
            struct((RANK, cols), f32),
            struct((RANK, width), f32),
        ],
        own.size,
        12 * own.size,
    )(own, back)


def shift(array, by):
    n = lax.axis_size("head")
    return lax.ppermute(array, "head", [(i, (i + by) % n) for i in range(n)])


def from_head(array):
    return [shift(array, by) for by in (2, 1, 3)]


def swap_cores(array):
    n = lax.axis_size("ctx")
    return lax.ppermute(array, "ctx", [(i, i ^ 1) for i in range(n)])


def chip_place():
    n = lax.axis_size("ctx")
    chip = lax.axis_index("ctx") // 2
    side = {32: 4}[n]
    return lax.rem(chip, side), chip // side


def along(array, axis, by):
    n = lax.axis_size("ctx")
    side = {32: 4}[n]
    pairs = []
    for i in range(n):
        core, x, z = i % 2, (i // 2) % side, i // (2 * side)
        if axis == "x":
            x = (x + by) % side
        else:
            z = (z + by) % side
        pairs.append((i, (z * side + x) * 2 + core))
    return lax.ppermute(array, "ctx", pairs)


def from_axis(array, axis):
    return [along(array, axis, by) for by in (1, 3, 2)]


def pair_kernel(mine_ref, got_ref, out_ref):
    out_ref[...] = (mine_ref[...] + got_ref[...].astype(f32)).astype(bf16)


def before_sum(reverse, place, refs):
    total = jnp.zeros(refs[0].shape, f32)
    for by, ref in zip((1, 3, 2), refs):
        wanted = (place < by) if reverse else (place >= by)
        total = total + jnp.where(wanted, ref[...].astype(f32), 0.0)
    return total


def row_kernel(reverse, mine_ref, got_ref, one_ref, three_ref, two_ref, *refs):
    row_ref, before_ref = refs[-2:]
    others = (one_ref, three_ref, two_ref)
    total = mine_ref[...] + got_ref[...].astype(f32)
    for ref in others:
        total = total + ref[...].astype(f32)
    row_ref[...] = total.astype(bf16)
    before_ref[...] = before_sum(reverse, chip_place()[0], others)


def combine_kernel(
    reverse, mine_ref, got_ref, before_ref, one_ref, three_ref, two_ref, *refs
):
    own_ref, other_ref = refs[-2:]
    chip = before_ref[...] + before_sum(reverse, chip_place()[1], (one_ref, three_ref, two_ref))
    first = first_core() != reverse
    own_ref[...] = jnp.where(first, chip, chip + got_ref[...].astype(f32)).astype(bf16)
    other_ref[...] = jnp.where(first, chip + mine_ref[...], chip).astype(bf16)


def glue(kernel, operands, out_dtypes, unread=()):
    shape = operands[0].shape
    return call(
        kernel,
        [IN_VMEM] * len(operands) + [UNREAD] * len(unread),
        [struct(shape, dtype) for dtype in out_dtypes],
        operands[0].size,
        8 * operands[0].size,
    )(*operands, *unread)


def scan_pair(mine, given):
    got = swap_cores(given)
    return glue(pair_kernel, [mine, got], [bf16])[0], got


def scan_row(mine, got, arrived, reverse, during):
    row, before = glue(
        functools.partial(row_kernel, reverse), [mine, got] + arrived, [bf16, f32], during
    )
    return mine, got, row, before


def scan_rest(middle, arrived, reverse, during):
    mine, got, _, before = middle
    own, other = glue(
        functools.partial(combine_kernel, reverse),
        [mine, got, before] + arrived,
        [bf16, bf16],
        during,
    )
    return own, swap_cores(other)


def row_sum_kernel(count, mine_ref, *refs):
    total = mine_ref[...].astype(f32)
    for ref in refs[:count]:
        total = total + ref[...].astype(f32)
    refs[-1][...] = total.astype(bf16)


def sum_pair(mine, given):
    got = swap_cores(given)
    return glue(functools.partial(row_sum_kernel, 1), [mine, got], [bf16])[0], got


def sum_row(mine, got, arrived, during):
    return glue(
        functools.partial(row_sum_kernel, 4), [mine, got] + arrived, [bf16], during
    )[0]


def sum_rest(row):
    (total,) = glue(functools.partial(row_sum_kernel, 3), [row] + from_axis(row, "z"), [bf16])
    return total, swap_cores(total)


def on_device(
    tokens,
    query_key_value_weight,
    output_weight,
    input_down_weights,
    input_up_weights,
    output_down_weight,
    output_up_weight,
    cotangent,
):
    rows, width = tokens.shape
    cols = query_key_value_weight.shape[2]
    n = lax.axis_size("ctx")
    scale_factor = adapter_scale * (rows * n) ** (-0.5)
    down_t = input_down_weights.transpose(0, 2, 1).reshape(3 * RANK, width)
    down_out_t = output_down_weight.T

    weight = query_key_value_weight

    top, bottom = start(tokens, down_t)
    one_top, three_bottom = shift(top, 1), shift(bottom, 3)
    one_bottom, three_top = shift(bottom, 1), shift(top, 3)
    two = shift(one_top, 1), shift(three_bottom, 3)
    total = project_first(tokens, weight)
    total = project_next(1, (one_top, one_bottom), total, weight, width)
    total = project_next(3, (three_top, three_bottom), total, weight, width)
    cot_own = cotangent_parts(cotangent, output_up_weight, total)
    cot_one, cot_three = shift(cot_own, 1), shift(cot_own, 3)
    qkv, mine, given, low = project_last(
        two, total, (top, one_top, three_top), input_up_weights, weight, width
    )

    pair, got = scan_pair(mine, given)
    scores, raw = inside_forward(qkv, pair)
    arrived = from_axis(pair, "x")
    cot_top, cot_bottom = halves(cot_one, cot_three, arrived[0])
    cot_two = shift(cot_top, 1), shift(cot_bottom, 3)
    middle = scan_row(mine, got, arrived, False, [raw, cot_top])
    grad, back_mid = attended_gradient(
        [cot_own, cot_one, cot_three, *cot_two], down_out_t, output_weight
    )
    held = scan_rest(middle, from_axis(middle[2], "z"), False, [])

    attended, d_raw, mine, given = forward_heads(qkv, raw, held, grad)
    pair, got = scan_pair(mine, given)
    dq, dk_within, dv_within, back_q, mid, early = within_block(
        qkv, scores, held, d_raw, attended, back_mid, low, input_up_weights, down_out_t, pair
    )
    arrived = from_axis(pair, "x")
    far_top, far_bottom = output_far(attended, output_weight, width, [arrived[0], early])
    relays = shift(far_top, 1), shift(far_bottom, 3)
    middle = scan_row(mine, got, arrived, True, [early, far_top])
    dq_parts = query_part(dq, weight, width, middle[2])
    out_own, out_one, out_three = output_near(attended, relays, output_weight, middle[2])
    out_got = shift(out_one, 1), shift(out_three, 3)
    suffix = scan_rest(middle, from_axis(middle[2], "z"), True, [dq_parts, out_own])

    dkv, back_part = across_blocks(
        qkv, suffix, dk_within, dv_within, back_q, mid, input_up_weights
    )
    back_got = from_head(back_part)
    piece, near = struct((rows, width), bf16), struct((rows, width), f32)

    def sent(by, unread):
        kernel = functools.partial(input_piece_kernel, by)
        part = input_call(kernel, dkv, dq_parts, weight, piece, unread)
        return part, shift(part, by)

    part_two, got_two = sent(2, back_got[0])
    part_one, got_one = sent(1, part_two)
    part_three, got_three = sent(3, part_one)
    back_low, mine, given = grads(
        [back_part] + back_got, tokens, cotangent, low, dkv, early, [part_three]
    )
    pair, got = sum_pair(mine, given)
    row = sum_row(mine, got, from_axis(pair, "x"), [got_two])
    grad_own = input_call(input_own_kernel, dkv, dq_parts, weight, near, row)
    output = output_sum(out_own, out_got, back_low, output_up_weight, row)
    grad_got = [got_two, got_one, got_three]
    sums = sum_rest(row)
    input_grad = input_sum(grad_own, grad_got, back_low, down_t)
    grad_down_qkv, grad_up_qkv, grad_down_out, grad_up_out = unpack(
        *sums, scale_factor, width, cols
    )
    return (
        output,
        input_grad,
        grad_down_qkv.transpose(0, 2, 1),
        grad_up_qkv,
        grad_down_out.T,
        grad_up_out,
    )


def solution(mesh):
    return jax.shard_map(
        on_device,
        mesh=mesh,
        in_specs=(
            P("ctx", "head"),
            P(None, None, "head"),
            P("head", None),
            P(None, "head", None),
            P(None, None, "head"),
            P("head", None),
            P(None, "head"),
            P("ctx", "head"),
        ),
        out_specs=(
            P("ctx", "head"),
            P("ctx", "head"),
            P(None, "head", None),
            P(None, None, "head"),
            P("head", None),
            P(None, "head"),
        ),
        check_vma=False,
    )
```

```python
import functools

import jax
import jax.numpy as jnp
from jax import lax
from jax.experimental import pallas as pl
from jax.experimental.pallas import tpu as pltpu
from jax.sharding import PartitionSpec as P

HEAD_DIM = 128
RANK = 16
TILE = 256
LANES = 128
adapter_scale = 0.5
epsilon = 1e-06
bf16 = jnp.bfloat16
f32 = jnp.float32
HINT = 2 * 10**10
VMEM_BYTES = 12 * 2**20

NN = (((1,), (0,)), ((), ()))
NT = (((1,), (1,)), ((), ()))
TN = (((0,), (0,)), ((), ()))

IN_HBM = pl.BlockSpec(memory_space=pltpu.HBM)
IN_VMEM = pl.BlockSpec(memory_space=pltpu.VMEM)
UNREAD = pl.BlockSpec(memory_space=pl.ANY)


def mm(a, b, dims=NN):
    return lax.dot_general(a, b, dims, preferred_element_type=f32)


def struct(shape, dtype):
    return jax.ShapeDtypeStruct(shape, dtype)


def call(kernel, specs, out_shape, flops, moved, scratch=(), aliases=None):
    many = isinstance(out_shape, (list, tuple))
    return pl.pallas_call(
        kernel,
        in_specs=specs,
        out_specs=[IN_VMEM] * len(out_shape) if many else IN_VMEM,
        out_shape=out_shape,
        scratch_shapes=list(scratch),
        input_output_aliases=aliases or {},
        compiler_params=pltpu.CompilerParams(vmem_limit_bytes=VMEM_BYTES),
        cost_estimate=pl.CostEstimate(flops=flops, bytes_accessed=moved, transcendentals=0),
    )


def member(shift):
    return lax.rem(lax.axis_index("head") + shift + 4, 4)


def first_core():
    return lax.rem(lax.axis_index("ctx"), 2) == 0


def chunk_rows(weight_ref, m, shift, width):
    return weight_ref[m, pl.ds(pl.multiple_of(member(shift) * width, width), width)]


def start_kernel(tok_ref, down_ref, top_ref, bottom_ref):
    half = top_ref.shape[0]
    width = tok_ref.shape[1]
    top_ref[:, :width] = tok_ref[:half]
    bottom_ref[:, :width] = tok_ref[half:]
    small = mm(tok_ref[...], down_ref[...], NT)
    value = small.astype(bf16)
    rest = (small - value.astype(f32)).astype(bf16)
    pad = jnp.zeros((half, LANES - 6 * RANK), bf16)
    small = jnp.concatenate(
        [value[:half], rest[:half], pad, value[half:], rest[half:], pad], axis=1
    )
    top_ref[:, width:] = small
    bottom_ref[:, width:] = small


def start(tok, down_t):
    rows, width = tok.shape
    return call(
        start_kernel,
        [IN_VMEM] * 2,
        [struct((rows // 2, width + 2 * LANES), bf16)] * 2,
        HINT,
        6 * rows * width,
    )(tok, down_t)


def project_first_kernel(tok_ref, weight_ref, total_ref):
    for m in range(3):
        total_ref[m] = mm(tok_ref[...], chunk_rows(weight_ref, m, 0, tok_ref.shape[1]))


def project_first(tok, weight):
    rows, width = tok.shape
    cols = weight.shape[2]
    return call(
        project_first_kernel,
        [IN_VMEM] * 2,
        struct((3, rows, cols), f32),
        6 * rows * width * cols,
        6 * width * cols,
    )(tok, weight)


def joined(buffer, top_ref, bottom_ref):
    half = top_ref.shape[0]
    buffer[:half] = top_ref[:, : buffer.shape[1]]
    buffer[half:] = bottom_ref[:, : buffer.shape[1]]
    return buffer[...]


def project_next_kernel(by, top_ref, bottom_ref, sum_ref, weight_ref, total_ref, buffer):
    tok = joined(buffer, top_ref, bottom_ref)
    for m in range(3):
        total_ref[m] = sum_ref[m] + mm(tok, chunk_rows(weight_ref, m, -by, tok.shape[1]))


def project_next(by, halves, total, weight, width):
    _, rows, cols = total.shape
    return call(
        functools.partial(project_next_kernel, by),
        [IN_VMEM] * 4,
        struct((3, rows, cols), f32),
        6 * rows * width * cols,
        6 * width * cols,
        [pltpu.VMEM((rows, width), bf16)],
        {2: 0},
    )(*halves, total, weight)


def cotangent_kernel(cot_ref, out_up_ref, unread, out_ref):
    rows, width = cot_ref.shape
    out_ref[:, :width] = cot_ref[...]
    back = mm(cot_ref[...], out_up_ref[...], NT).astype(bf16)
    out_ref[:, width:] = jnp.concatenate(
        [back, jnp.zeros((rows, LANES - RANK), bf16)], axis=1
    )


def cotangent_parts(cot, out_up, unread):
    rows, width = cot.shape
    return call(
        cotangent_kernel,
        [IN_VMEM] * 2 + [UNREAD],
        struct((rows, width + LANES), bf16),
        2 * rows * width * RANK,
        4 * rows * width,
    )(cot, out_up, unread)


def split_states(state, mine_ref, given_ref):
    half = mine_ref.shape[0]
    first = first_core()
    for h in range(half):
        low, high = state[h], state[half + h]
        mine_ref[h] = jnp.where(first, low, high)
        given_ref[h] = jnp.where(first, high, low).astype(bf16)


def project_last_kernel(
    top_ref, bottom_ref, sum_ref, own_ref, one_ref, three_ref, up_ref, weight_ref,
    qkv_ref, mine_ref, given_ref, low_ref, state, buffer,
):
    tok = joined(buffer, top_ref, bottom_ref)
    half = top_ref.shape[0]
    width = tok.shape[1]
    low = sum(
        ref[:, width:].astype(f32) for ref in (own_ref, one_ref, three_ref, top_ref)
    )
    for at, part in ((slice(0, half), low[:, :LANES]), (slice(half, 2 * half), low[:, LANES:])):
        low_ref[at] = (part[:, : 3 * RANK] + part[:, 3 * RANK : 6 * RANK]).astype(bf16)
    for m in (1, 2, 0):
        total = sum_ref[m] + mm(tok, chunk_rows(weight_ref, m, -2, width))
        total = total + adapter_scale * mm(low_ref[:, m * RANK : (m + 1) * RANK], up_ref[m])
        qkv_ref[m] = total.astype(bf16)
    for h in range(state.shape[0]):
        at = slice(h * HEAD_DIM, (h + 1) * HEAD_DIM)
        state[h] = mm(qkv_ref[1, :, at], qkv_ref[2, :, at], TN)
    split_states(state, mine_ref, given_ref)


def project_last(halves, total, smalls, up, weight, width):
    _, rows, cols = total.shape
    heads = cols // HEAD_DIM
    square = (HEAD_DIM, HEAD_DIM)
    return call(
        project_last_kernel,
        [IN_VMEM] * 8,
        [
            struct((3, rows, cols), bf16),
            struct((heads // 2,) + square, f32),
            struct((heads // 2,) + square, bf16),
            struct((rows, 3 * RANK), bf16),
        ],
        6 * rows * width * cols,
        6 * width * cols,
        [pltpu.VMEM((heads,) + square, f32), pltpu.VMEM((rows, width), bf16)],
    )(*halves, total, *smalls, up, weight)


def attended_gradient_kernel(
    cot0, cot1, cot3, top_ref, bottom_ref, down_ref, weight_ref, out_ref, back_ref, buffer
):
    width = cot0.shape[1] - LANES
    joined(buffer, top_ref, bottom_ref)
    refs = ((0, cot0), (1, cot1), (3, cot3), (2, buffer))
    back = sum(ref[:, width:].astype(f32) for _, ref in refs).astype(bf16)[:, :RANK]
    back_ref[...] = back
    total = adapter_scale * mm(back, down_ref[...])
    for by, ref in refs:
        chunk = pl.ds(pl.multiple_of(member(-by) * width, width), width)
        total = total + mm(ref[:, :width], weight_ref[:, chunk], NT)
    out_ref[...] = total


def attended_gradient(cots, down_out, weight):
    rows, wide = cots[0].shape
    cols, full = weight.shape
    return call(
        attended_gradient_kernel,
        [IN_VMEM] * 7,
        [struct((rows, cols), f32), struct((rows, RANK), bf16)],
        2 * rows * full * cols,
        2 * full * cols,
        [pltpu.VMEM((rows, wide), bf16)],
    )(*cots, down_out, weight)


def lower_mask(rows):
    s = lax.broadcasted_iota(jnp.int32, (rows, rows), 0)
    t = lax.broadcasted_iota(jnp.int32, (rows, rows), 1)
    return s >= t


def lanes_of(h):
    return slice(h * HEAD_DIM, (h + 1) * HEAD_DIM)


def held_of(own_ref, back_ref, h):
    half = own_ref.shape[0]
    i = h % half
    if h < half:
        return jnp.where(first_core(), own_ref[i], back_ref[i])
    return jnp.where(first_core(), back_ref[i], own_ref[i])


def inside_kernel(qkv_ref, unread, scores_ref, raw_ref):
    mask = lower_mask(raw_ref.shape[0])
    for h in range(scores_ref.shape[0]):
        q, k, v = (qkv_ref[m, :, lanes_of(h)] for m in range(3))
        scores = jnp.where(mask, mm(q, k, NT), 0.0).astype(bf16)
        scores_ref[h] = scores
        raw_ref[:, lanes_of(h)] = mm(scores, v)


def inside_forward(qkv, unread):
    _, rows, cols = qkv.shape
    heads = cols // HEAD_DIM
    return call(
        inside_kernel,
        [IN_VMEM, UNREAD],
        [struct((heads, rows, rows), bf16), struct((rows, cols), f32)],
        4 * rows * cols * rows,
        6 * rows * cols,
    )(qkv, unread)


def halves_kernel(one_ref, three_ref, unread, top_ref, bottom_ref):
    half = top_ref.shape[0]
    top_ref[...] = one_ref[:half]
    bottom_ref[...] = three_ref[half:]


def halves(one, three, unread):
    rows, width = one.shape
    return call(
        halves_kernel,
        [IN_VMEM] * 2 + [UNREAD],
        [struct((rows // 2, width), bf16)] * 2,
        rows * width,
        4 * rows * width,
    )(one, three, unread)


def forward_kernel(
    qkv_ref, raw_ref, own_ref, back_ref, grad_ref, att_ref, draw_ref, mine_ref, given_ref, state
):
    for h in range(state.shape[0]):
        at = lanes_of(h)
        q = qkv_ref[0, :, at]
        raw = raw_ref[:, at] + mm(q, held_of(own_ref, back_ref, h))
        inverse = lax.rsqrt(jnp.mean(raw * raw, axis=-1, keepdims=True) + epsilon)
        normed = raw * inverse
        att_ref[:, at] = normed.astype(bf16)
        grad = grad_ref[:, at]
        along = jnp.mean(grad * normed, axis=-1, keepdims=True)
        draw = ((grad - normed * along) * inverse).astype(bf16)
        draw_ref[:, at] = draw
        state[h] = mm(q, draw, TN)
    split_states(state, mine_ref, given_ref)


def forward_heads(qkv, raw, held, grad):
    _, rows, cols = qkv.shape
    heads = cols // HEAD_DIM
    square = (HEAD_DIM, HEAD_DIM)
    return call(
        forward_kernel,
        [IN_VMEM] * 5,
        [
            struct((rows, cols), bf16),
            struct((rows, cols), bf16),
            struct((heads // 2,) + square, f32),
            struct((heads // 2,) + square, bf16),
        ],
        8 * rows * cols * HEAD_DIM,
        14 * rows * cols,
        [pltpu.VMEM((heads,) + square, f32)],
    )(qkv, raw, *held, grad)


def to_blocks(out_ref, base, rows):
    for b in range(rows.shape[1] // LANES):
        out_ref[base + b] = rows[:, b * LANES : (b + 1) * LANES]


def within_kernel(
    qkv_ref, scores_ref, own_ref, back_ref, draw_ref, att_ref, back_mid_ref, low_ref, up_ref,
    down_ref, unread, dq_ref, dk_ref, dv_ref, back_q_ref, mid_ref, early_ref,
):
    rows = draw_ref.shape[0]
    heads = scores_ref.shape[0]
    mask = lower_mask(rows)
    for h in range(heads):
        at = lanes_of(h)
        q, k, v = (qkv_ref[m, :, at] for m in range(3))
        draw = draw_ref[:, at]
        dscores = jnp.where(mask, mm(draw, v, NT), 0.0).astype(bf16)
        dq = mm(dscores, k) + mm(draw, held_of(own_ref, back_ref, h), NT)
        dq_ref[:, at] = dq.astype(bf16)
        dk_ref[:, at] = mm(dscores, q, TN)
        dv_ref[:, at] = mm(scores_ref[h], draw, TN)
    back_q_ref[...] = mm(dq_ref[...], up_ref[0], NT)
    mid_ref[...] = mm(att_ref[...], down_ref[...], NT)
    to_blocks(early_ref, 0, mm(back_mid_ref[...], att_ref[...], TN))
    to_blocks(early_ref, heads, mm(low_ref[:, :RANK], dq_ref[...], TN))


def within_block(qkv, scores, held, draw, att, back_mid, low, up, down_out, unread):
    _, rows, cols = qkv.shape
    heads = cols // HEAD_DIM
    return call(
        within_kernel,
        [IN_VMEM] * 10 + [UNREAD],
        [
            struct((rows, cols), bf16),
            struct((rows, cols), f32),
            struct((rows, cols), f32),
            struct((rows, RANK), f32),
            struct((rows, RANK), f32),
            struct((2 * heads, RANK, LANES), f32),
        ],
        4 * rows * cols * (4 * rows),
        18 * rows * cols,
    )(qkv, scores, *held, draw, att, back_mid, low, up, down_out, unread)


def across_kernel(
    qkv_ref, own_ref, back_ref, dk_ref, dv_ref, back_q_ref, mid_ref, up_ref, unread, out_ref, low_ref
):
    for h in range(out_ref.shape[2] // HEAD_DIM):
        at = lanes_of(h)
        held = held_of(own_ref, back_ref, h)
        out_ref[0, :, at] = (dk_ref[:, at] + mm(qkv_ref[2, :, at], held, NT)).astype(bf16)
        out_ref[1, :, at] = (dv_ref[:, at] + mm(qkv_ref[1, :, at], held)).astype(bf16)
    low_ref[:, :RANK] = back_q_ref[...].astype(bf16)
    low_ref[:, 3 * RANK :] = mid_ref[...].astype(bf16)
    for m in (1, 2):
        low_ref[:, m * RANK : (m + 1) * RANK] = mm(out_ref[m - 1], up_ref[m], NT).astype(bf16)


def across_blocks(qkv, held, dk, dv, back_q, mid, up, unread):
    _, rows, cols = qkv.shape
    return call(
        across_kernel,
        [IN_VMEM] * 8 + [UNREAD],
        [struct((2, rows, cols), bf16), struct((rows, 4 * RANK), bf16)],
        8 * rows * cols * HEAD_DIM,
        18 * rows * cols,
    )(qkv, *held, dk, dv, back_q, mid, up, unread)


def output_product(by, att_ref, weight_ref, width):
    chunk = pl.ds(pl.multiple_of(member(by) * width, width), width)
    return mm(att_ref[...], weight_ref[:, chunk])


def output_far_kernel(att_ref, weight_ref, top_ref, bottom_ref):
    half, width = top_ref.shape
    part = output_product(2, att_ref, weight_ref, width).astype(bf16)
    top_ref[...] = part[:half]
    bottom_ref[...] = part[half:]


def output_far(att, weight, width):
    rows, cols = att.shape
    return call(
        output_far_kernel,
        [IN_VMEM] * 2,
        [struct((rows // 2, width), bf16)] * 2,
        2 * rows * cols * width,
        2 * cols * width,
    )(att, weight)


def output_near_kernel(
    att_ref, relay_top, relay_bottom, weight_ref, unread, own_ref, one_ref, three_ref
):
    half, width = relay_top.shape
    own_ref[...] = output_product(0, att_ref, weight_ref, width)
    one = output_product(1, att_ref, weight_ref, width)
    one_ref[:half] = (one[:half] + relay_top[...].astype(f32)).astype(bf16)
    one_ref[half:] = one[half:].astype(bf16)
    three = output_product(3, att_ref, weight_ref, width)
    three_ref[:half] = three[:half].astype(bf16)
    three_ref[half:] = (three[half:] + relay_bottom[...].astype(f32)).astype(bf16)


def output_near(att, relays, weight, unread):
    rows, cols = att.shape
    width = relays[0].shape[1]
    return call(
        output_near_kernel,
        [IN_VMEM] * 4 + [UNREAD],
        [struct((rows, width), f32)] + [struct((rows, width), bf16)] * 2,
        6 * rows * cols * width,
        6 * cols * width,
    )(att, *relays, weight, unread)


def output_merge_kernel(own_ref, one_ref, three_ref, unread, out_ref):
    out_ref[...] = own_ref[...] + one_ref[...].astype(f32) + three_ref[...].astype(f32)


def output_merge(own, parts, unread):
    return call(
        output_merge_kernel,
        [IN_VMEM] * 3 + [UNREAD],
        struct(own.shape, f32),
        2 * own.size,
        12 * own.size,
    )(own, *parts, unread)


def output_sum_kernel(merged_ref, low_ref, up_ref, unread, out_ref):
    total = merged_ref[...] + adapter_scale * mm(low_ref[:, 3 * RANK :], up_ref[...])
    out_ref[...] = total.astype(bf16)


def output_sum(merged, low, up, unread):
    rows, width = merged.shape
    return call(
        output_sum_kernel,
        [IN_VMEM] * 3 + [UNREAD],
        struct((rows, width), bf16),
        2 * rows * width * RANK,
        6 * rows * width,
    )(merged, low, up, unread)


def query_kernel(dq_ref, weight_ref, unread, out_ref):
    parts, _, width = out_ref.shape
    for p in range(parts):
        out_ref[p] = mm(dq_ref[...], weight_ref[0, p * width : (p + 1) * width], NT)


def query_part(dq, weight, width, unread):
    rows, cols = dq.shape
    parts = weight.shape[1] // width
    return call(
        query_kernel,
        [IN_VMEM] * 2 + [UNREAD],
        struct((parts, rows, width), f32),
        2 * rows * cols * width * parts,
        2 * cols * width * parts,
    )(dq, weight, unread)


def input_product(by, dkv_ref, dq_ref, weight_ref):
    total = dq_ref[member(by)]
    for m in range(2):
        total = total + mm(
            dkv_ref[m], chunk_rows(weight_ref, m + 1, by, total.shape[1]), NT
        )
    return total


def input_piece_kernel(by, dkv_ref, dq_ref, weight_ref, unread, out_ref):
    out_ref[...] = input_product(by, dkv_ref, dq_ref, weight_ref).astype(bf16)


def input_own_kernel(dkv_ref, dq_ref, weight_ref, unread, out_ref):
    out_ref[...] = input_product(0, dkv_ref, dq_ref, weight_ref)


def input_call(kernel, dkv, dq_parts, weight, out, *more):
    _, rows, cols = dkv.shape
    width = dq_parts.shape[2]
    return call(
        kernel,
        [IN_VMEM] * 3 + [UNREAD] * len(more),
        out,
        4 * rows * cols * width,
        4 * cols * width,
    )(dkv, dq_parts, weight, *more)


def input_sum_kernel(own_ref, two_ref, one_ref, three_ref, low_ref, down_ref, out_ref):
    total = own_ref[...] + adapter_scale * mm(low_ref[:, : 3 * RANK], down_ref[...])
    for ref in (two_ref, one_ref, three_ref):
        total = total + ref[...].astype(f32)
    out_ref[...] = total.astype(bf16)


def input_sum(own, parts, low, down_t):
    rows, width = own.shape
    return call(
        input_sum_kernel,
        [IN_VMEM] * 6,
        struct((rows, width), bf16),
        6 * rows * width * RANK,
        12 * rows * width,
    )(own, *parts, low, down_t)


def grads_kernel(
    back0, back2, back1, back3, tok_ref, cot_ref, low_ref, dkv_ref, early_ref,
    *refs,
):
    back_ref, mine_ref, given_ref, packed = refs[-4:]
    back = back0[...].astype(f32) + back2[...].astype(f32)
    back = (back + back1[...].astype(f32) + back3[...].astype(f32)).astype(bf16)
    back_ref[...] = back
    down = mm(back[:, : 3 * RANK], tok_ref[...], TN)
    up_out = mm(back[:, 3 * RANK :], cot_ref[...], TN)
    at = 0
    for m in range(3):
        to_blocks(packed, at, down[m * RANK : (m + 1) * RANK])
        at += tok_ref.shape[1] // LANES
    to_blocks(packed, at, up_out)
    at += cot_ref.shape[1] // LANES
    packed[at : at + early_ref.shape[0]] = early_ref[...]
    at += early_ref.shape[0]
    for m in (1, 2):
        to_blocks(packed, at, mm(low_ref[:, m * RANK : (m + 1) * RANK], dkv_ref[m - 1], TN))
        at += dkv_ref.shape[2] // LANES
    half = mine_ref.shape[0]
    first = first_core()
    mine_ref[...] = jnp.where(first, packed[:half], packed[half:])
    given_ref[...] = jnp.where(first, packed[half:], packed[:half]).astype(bf16)


def grads(backs, tokens, cot, low, dkv, early, unread):
    rows, width = tokens.shape
    cols = dkv.shape[2]
    half = 2 * (width + cols) // LANES
    return call(
        grads_kernel,
        [IN_VMEM] * 9 + [UNREAD] * len(unread),
        [
            struct(backs[0].shape, bf16),
            struct((half, RANK, LANES), f32),
            struct((half, RANK, LANES), bf16),
        ],
        2 * rows * RANK * (3 * width + 2 * cols),
        2 * dkv.size + 2 * tokens.size,
        [pltpu.VMEM((2 * half, RANK, LANES), f32)],
    )(*backs, tokens, cot, low, dkv, early, *unread)


def unpack_kernel(scale, own_ref, back_ref, down_ref, up_ref, down_out_ref, up_out_ref):
    half = own_ref.shape[0]
    at = 0

    def take(count):
        nonlocal at
        at += count
        first = first_core()
        blocks = []
        for b in range(at - count, at):
            own, back = own_ref[b % half], back_ref[b % half]
            block = jnp.where(first, own, back) if b < half else jnp.where(first, back, own)
            blocks.append(block.astype(f32))
        return scale * jnp.concatenate(blocks, axis=1)

    wide, heads = up_out_ref.shape[1] // LANES, down_out_ref.shape[1] // LANES
    for m in range(3):
        down_ref[m] = take(wide)
    up_out_ref[...] = take(wide)
    down_out_ref[...] = take(heads)
    for m in range(3):
        up_ref[m] = take(heads)


def unpack(own, back, scale, width, cols):
    return call(
        functools.partial(unpack_kernel, scale),
        [IN_VMEM] * 2,
        [
            struct((3, RANK, width), f32),
            struct((3, RANK, cols), f32),
            struct((RANK, cols), f32),
            struct((RANK, width), f32),
        ],
        own.size,
        12 * own.size,
    )(own, back)


def shift(array, by):
    n = lax.axis_size("head")
    return lax.ppermute(array, "head", [(i, (i + by) % n) for i in range(n)])


def from_head(array):
    return [shift(array, by) for by in (2, 1, 3)]


def swap_cores(array):
    n = lax.axis_size("ctx")
    return lax.ppermute(array, "ctx", [(i, i ^ 1) for i in range(n)])


def chip_place():
    n = lax.axis_size("ctx")
    chip = lax.axis_index("ctx") // 2
    side = {32: 4}[n]
    return lax.rem(chip, side), chip // side


def along(array, axis, by):
    n = lax.axis_size("ctx")
    side = {32: 4}[n]
    pairs = []
    for i in range(n):
        core, x, z = i % 2, (i // 2) % side, i // (2 * side)
        if axis == "x":
            x = (x + by) % side
        else:
            z = (z + by) % side
        pairs.append((i, (z * side + x) * 2 + core))
    return lax.ppermute(array, "ctx", pairs)


def from_axis(array, axis):
    return [along(array, axis, by) for by in (1, 3, 2)]


def pair_kernel(mine_ref, got_ref, out_ref):
    out_ref[...] = (mine_ref[...] + got_ref[...].astype(f32)).astype(bf16)


def before_sum(reverse, place, refs):
    total = jnp.zeros(refs[0].shape, f32)
    for by, ref in zip((1, 3, 2), refs):
        wanted = (place < by) if reverse else (place >= by)
        total = total + jnp.where(wanted, ref[...].astype(f32), 0.0)
    return total


def row_kernel(reverse, mine_ref, got_ref, one_ref, three_ref, two_ref, *refs):
    row_ref, before_ref = refs[-2:]
    others = (one_ref, three_ref, two_ref)
    total = mine_ref[...] + got_ref[...].astype(f32)
    for ref in others:
        total = total + ref[...].astype(f32)
    row_ref[...] = total.astype(bf16)
    before_ref[...] = before_sum(reverse, chip_place()[0], others)


def combine_kernel(
    reverse, mine_ref, got_ref, before_ref, one_ref, three_ref, two_ref, *refs
):
    own_ref, other_ref = refs[-2:]
    chip = before_ref[...] + before_sum(reverse, chip_place()[1], (one_ref, three_ref, two_ref))
    first = first_core() != reverse
    own_ref[...] = jnp.where(first, chip, chip + got_ref[...].astype(f32)).astype(bf16)
    other_ref[...] = jnp.where(first, chip + mine_ref[...], chip).astype(bf16)


def glue(kernel, operands, out_dtypes, unread=()):
    shape = operands[0].shape
    return call(
        kernel,
        [IN_VMEM] * len(operands) + [UNREAD] * len(unread),
        [struct(shape, dtype) for dtype in out_dtypes],
        operands[0].size,
        8 * operands[0].size,
    )(*operands, *unread)


def scan_pair(mine, given):
    got = swap_cores(given)
    return glue(pair_kernel, [mine, got], [bf16])[0], got


def scan_row(mine, got, arrived, reverse, during):
    row, before = glue(
        functools.partial(row_kernel, reverse), [mine, got] + arrived, [bf16, f32], during
    )
    return mine, got, row, before


def scan_rest(middle, arrived, reverse, during):
    mine, got, _, before = middle
    own, other = glue(
        functools.partial(combine_kernel, reverse),
        [mine, got, before] + arrived,
        [bf16, bf16],
        during,
    )
    return own, swap_cores(other)


def row_sum_kernel(count, mine_ref, *refs):
    total = mine_ref[...].astype(f32)
    for ref in refs[:count]:
        total = total + ref[...].astype(f32)
    refs[-1][...] = total.astype(bf16)


def sum_pair(mine, given):
    got = swap_cores(given)
    return glue(functools.partial(row_sum_kernel, 1), [mine, got], [bf16])[0], got


def sum_row(mine, got, arrived, during):
    return glue(
        functools.partial(row_sum_kernel, 4), [mine, got] + arrived, [bf16], during
    )[0]


def sum_rest(row, during):
    (total,) = glue(
        functools.partial(row_sum_kernel, 3), [row] + from_axis(row, "z"), [bf16], during
    )
    return total, swap_cores(total)


def on_device(
    tokens,
    query_key_value_weight,
    output_weight,
    input_down_weights,
    input_up_weights,
    output_down_weight,
    output_up_weight,
    cotangent,
):
    rows, width = tokens.shape
    cols = query_key_value_weight.shape[2]
    n = lax.axis_size("ctx")
    scale_factor = adapter_scale * (rows * n) ** (-0.5)
    down_t = input_down_weights.transpose(0, 2, 1).reshape(3 * RANK, width)
    down_out_t = output_down_weight.T

    weight = query_key_value_weight

    top, bottom = start(tokens, down_t)
    one_top, three_bottom = shift(top, 1), shift(bottom, 3)
    one_bottom, three_top = shift(bottom, 1), shift(top, 3)
    two = shift(one_top, 1), shift(three_bottom, 3)
    total = project_first(tokens, weight)
    total = project_next(1, (one_top, one_bottom), total, weight, width)
    total = project_next(3, (three_top, three_bottom), total, weight, width)
    cot_own = cotangent_parts(cotangent, output_up_weight, total)
    cot_one, cot_three = shift(cot_own, 1), shift(cot_own, 3)
    qkv, mine, given, low = project_last(
        two, total, (top, one_top, three_top), input_up_weights, weight, width
    )

    pair, got = scan_pair(mine, given)
    scores, raw = inside_forward(qkv, pair)
    arrived = from_axis(pair, "x")
    cot_top, cot_bottom = halves(cot_one, cot_three, arrived[0])
    cot_two = shift(cot_top, 1), shift(cot_bottom, 3)
    middle = scan_row(mine, got, arrived, False, [raw, cot_top])
    grad, back_mid = attended_gradient(
        [cot_own, cot_one, cot_three, *cot_two], down_out_t, output_weight
    )
    held = scan_rest(middle, from_axis(middle[2], "z"), False, [])

    attended, d_raw, mine, given = forward_heads(qkv, raw, held, grad)
    pair, got = scan_pair(mine, given)
    far_top, far_bottom = output_far(attended, output_weight, width)
    relays = shift(far_top, 1), shift(far_bottom, 3)
    out_own, out_one, out_three = output_near(attended, relays, output_weight, pair)
    out_got = shift(out_one, 1), shift(out_three, 3)
    middle = scan_row(mine, got, from_axis(pair, "x"), True, [out_own])
    dq, dk_within, dv_within, back_q, mid, early = within_block(
        qkv,
        scores,
        held,
        d_raw,
        attended,
        back_mid,
        low,
        input_up_weights,
        down_out_t,
        middle[2],
    )
    dq_parts = query_part(dq, weight, width, middle[2])
    merged = output_merge(out_own, out_got, early)
    suffix = scan_rest(middle, from_axis(middle[2], "z"), True, [dq_parts])

    dkv, back_part = across_blocks(
        qkv, suffix, dk_within, dv_within, back_q, mid, input_up_weights, merged
    )
    back_got = from_head(back_part)
    piece, near = struct((rows, width), bf16), struct((rows, width), f32)

    def sent(by, unread):
        kernel = functools.partial(input_piece_kernel, by)
        part = input_call(kernel, dkv, dq_parts, weight, piece, unread)
        return part, shift(part, by)

    part_two, got_two = sent(2, back_got[0])
    part_one, got_one = sent(1, part_two)
    part_three, got_three = sent(3, part_one)
    back_low, mine, given = grads(
        [back_part] + back_got, tokens, cotangent, low, dkv, early, [part_three]
    )
    pair, got = sum_pair(mine, given)
    row = sum_row(mine, got, from_axis(pair, "x"), [got_two])
    grad_own = input_call(input_own_kernel, dkv, dq_parts, weight, near, row)
    output = output_sum(merged, back_low, output_up_weight, row)
    grad_got = [got_two, got_one, got_three]
    sums = sum_rest(row, [grad_own, output])
    input_grad = input_sum(grad_own, grad_got, back_low, down_t)
    grad_down_qkv, grad_up_qkv, grad_down_out, grad_up_out = unpack(
        *sums, scale_factor, width, cols
    )
    return (
        output,
        input_grad,
        grad_down_qkv.transpose(0, 2, 1),
        grad_up_qkv,
        grad_down_out.T,
        grad_up_out,
    )


def solution(mesh):
    return jax.shard_map(
        on_device,
        mesh=mesh,
        in_specs=(
            P("ctx", "head"),
            P(None, None, "head"),
            P("head", None),
            P(None, "head", None),
            P(None, None, "head"),
            P("head", None),
            P(None, "head"),
            P("ctx", "head"),
        ),
        out_specs=(
            P("ctx", "head"),
            P("ctx", "head"),
            P(None, "head", None),
            P(None, None, "head"),
            P("head", None),
            P(None, "head"),
        ),
        check_vma=False,
    )
```

```python
import functools

import jax
import jax.numpy as jnp
from jax import lax
from jax.experimental import pallas as pl
from jax.experimental.pallas import tpu as pltpu
from jax.sharding import PartitionSpec as P

HEAD_DIM = 128
RANK = 16
TILE = 256
LANES = 128
adapter_scale = 0.5
epsilon = 1e-06
bf16 = jnp.bfloat16
f32 = jnp.float32
HINT = 2 * 10**10
VMEM_BYTES = 12 * 2**20

NN = (((1,), (0,)), ((), ()))
NT = (((1,), (1,)), ((), ()))
TN = (((0,), (0,)), ((), ()))

IN_HBM = pl.BlockSpec(memory_space=pltpu.HBM)
IN_VMEM = pl.BlockSpec(memory_space=pltpu.VMEM)
UNREAD = pl.BlockSpec(memory_space=pl.ANY)


def mm(a, b, dims=NN):
    return lax.dot_general(a, b, dims, preferred_element_type=f32)


def struct(shape, dtype):
    return jax.ShapeDtypeStruct(shape, dtype)


def call(kernel, specs, out_shape, flops, moved, scratch=(), aliases=None):
    many = isinstance(out_shape, (list, tuple))
    return pl.pallas_call(
        kernel,
        in_specs=specs,
        out_specs=[IN_VMEM] * len(out_shape) if many else IN_VMEM,
        out_shape=out_shape,
        scratch_shapes=list(scratch),
        input_output_aliases=aliases or {},
        compiler_params=pltpu.CompilerParams(vmem_limit_bytes=VMEM_BYTES),
        cost_estimate=pl.CostEstimate(flops=flops, bytes_accessed=moved, transcendentals=0),
    )


def member(shift):
    return lax.rem(lax.axis_index("head") + shift + 4, 4)


def first_core():
    return lax.rem(lax.axis_index("ctx"), 2) == 0


def chunk_rows(weight_ref, m, shift, width):
    return weight_ref[m, pl.ds(pl.multiple_of(member(shift) * width, width), width)]


def start_kernel(tok_ref, down_ref, top_ref, bottom_ref):
    half = top_ref.shape[0]
    width = tok_ref.shape[1]
    top_ref[:, :width] = tok_ref[:half]
    bottom_ref[:, :width] = tok_ref[half:]
    small = mm(tok_ref[...], down_ref[...], NT)
    value = small.astype(bf16)
    rest = (small - value.astype(f32)).astype(bf16)
    pad = jnp.zeros((half, LANES - 6 * RANK), bf16)
    small = jnp.concatenate(
        [value[:half], rest[:half], pad, value[half:], rest[half:], pad], axis=1
    )
    top_ref[:, width:] = small
    bottom_ref[:, width:] = small


def start(tok, down_t):
    rows, width = tok.shape
    return call(
        start_kernel,
        [IN_VMEM] * 2,
        [struct((rows // 2, width + 2 * LANES), bf16)] * 2,
        HINT,
        6 * rows * width,
    )(tok, down_t)


def project_first_kernel(tok_ref, weight_ref, total_ref):
    for m in range(3):
        total_ref[m] = mm(tok_ref[...], chunk_rows(weight_ref, m, 0, tok_ref.shape[1]))


def project_first(tok, weight):
    rows, width = tok.shape
    cols = weight.shape[2]
    return call(
        project_first_kernel,
        [IN_VMEM] * 2,
        struct((3, rows, cols), f32),
        6 * rows * width * cols,
        6 * width * cols,
    )(tok, weight)


def joined(buffer, top_ref, bottom_ref):
    half = top_ref.shape[0]
    buffer[:half] = top_ref[:, : buffer.shape[1]]
    buffer[half:] = bottom_ref[:, : buffer.shape[1]]
    return buffer[...]


def project_next_kernel(by, top_ref, bottom_ref, sum_ref, weight_ref, total_ref, buffer):
    tok = joined(buffer, top_ref, bottom_ref)
    for m in range(3):
        total_ref[m] = sum_ref[m] + mm(tok, chunk_rows(weight_ref, m, -by, tok.shape[1]))


def project_next(by, halves, total, weight, width):
    _, rows, cols = total.shape
    return call(
        functools.partial(project_next_kernel, by),
        [IN_VMEM] * 4,
        struct((3, rows, cols), f32),
        6 * rows * width * cols,
        6 * width * cols,
        [pltpu.VMEM((rows, width), bf16)],
        {2: 0},
    )(*halves, total, weight)


def cotangent_kernel(cot_ref, out_up_ref, unread, out_ref):
    rows, width = cot_ref.shape
    out_ref[:, :width] = cot_ref[...]
    back = mm(cot_ref[...], out_up_ref[...], NT).astype(bf16)
    out_ref[:, width:] = jnp.concatenate(
        [back, jnp.zeros((rows, LANES - RANK), bf16)], axis=1
    )


def cotangent_parts(cot, out_up, unread):
    rows, width = cot.shape
    return call(
        cotangent_kernel,
        [IN_VMEM] * 2 + [UNREAD],
        struct((rows, width + LANES), bf16),
        2 * rows * width * RANK,
        4 * rows * width,
    )(cot, out_up, unread)


def split_states(state, mine_ref, given_ref):
    half = mine_ref.shape[0]
    first = first_core()
    for h in range(half):
        low, high = state[h], state[half + h]
        mine_ref[h] = jnp.where(first, low, high)
        given_ref[h] = jnp.where(first, high, low).astype(bf16)


def project_last_kernel(
    top_ref, bottom_ref, sum_ref, own_ref, one_ref, three_ref, up_ref, weight_ref,
    qkv_ref, mine_ref, given_ref, low_ref, state, buffer,
):
    tok = joined(buffer, top_ref, bottom_ref)
    half = top_ref.shape[0]
    width = tok.shape[1]
    low = sum(
        ref[:, width:].astype(f32) for ref in (own_ref, one_ref, three_ref, top_ref)
    )
    for at, part in ((slice(0, half), low[:, :LANES]), (slice(half, 2 * half), low[:, LANES:])):
        low_ref[at] = (part[:, : 3 * RANK] + part[:, 3 * RANK : 6 * RANK]).astype(bf16)
    for m in (1, 2, 0):
        total = sum_ref[m] + mm(tok, chunk_rows(weight_ref, m, -2, width))
        total = total + adapter_scale * mm(low_ref[:, m * RANK : (m + 1) * RANK], up_ref[m])
        qkv_ref[m] = total.astype(bf16)
    for h in range(state.shape[0]):
        at = slice(h * HEAD_DIM, (h + 1) * HEAD_DIM)
        state[h] = mm(qkv_ref[1, :, at], qkv_ref[2, :, at], TN)
    split_states(state, mine_ref, given_ref)


def project_last(halves, total, smalls, up, weight, width):
    _, rows, cols = total.shape
    heads = cols // HEAD_DIM
    square = (HEAD_DIM, HEAD_DIM)
    return call(
        project_last_kernel,
        [IN_VMEM] * 8,
        [
            struct((3, rows, cols), bf16),
            struct((heads // 2,) + square, f32),
            struct((heads // 2,) + square, bf16),
            struct((rows, 3 * RANK), bf16),
        ],
        6 * rows * width * cols,
        6 * width * cols,
        [pltpu.VMEM((heads,) + square, f32), pltpu.VMEM((rows, width), bf16)],
    )(*halves, total, *smalls, up, weight)


def gradient_near_kernel(cot0, cot1, cot3, unread, weight_ref, out_ref, back_ref):
    width = cot0.shape[1] - LANES
    refs = ((0, cot0), (1, cot1), (3, cot3))
    back_ref[...] = sum(ref[:, width : width + RANK].astype(f32) for _, ref in refs)
    total = jnp.zeros(out_ref.shape, f32)
    for by, ref in refs:
        chunk = pl.ds(pl.multiple_of(member(-by) * width, width), width)
        total = total + mm(ref[:, :width], weight_ref[:, chunk], NT)
    out_ref[...] = total


def gradient_near(cots, weight, unread):
    rows = cots[0].shape[0]
    cols, full = weight.shape
    return call(
        gradient_near_kernel,
        [IN_VMEM] * 3 + [UNREAD, IN_VMEM],
        [struct((rows, cols), f32), struct((rows, RANK), f32)],
        3 * rows * full * cols // 2,
        2 * full * cols,
    )(*cots, unread, weight)


def gradient_far_kernel(
    top_ref, bottom_ref, near_ref, part_ref, down_ref, weight_ref, out_ref, back_ref, buffer
):
    width = buffer.shape[1] - LANES
    joined(buffer, top_ref, bottom_ref)
    back = (part_ref[...] + buffer[:, width : width + RANK].astype(f32)).astype(bf16)
    back_ref[...] = back
    chunk = pl.ds(pl.multiple_of(member(-2) * width, width), width)
    total = near_ref[...] + mm(buffer[:, :width], weight_ref[:, chunk], NT)
    out_ref[...] = total + adapter_scale * mm(back, down_ref[...])


def gradient_far(halves, near, part, down_out, weight):
    rows, cols = near.shape
    wide = halves[0].shape[1]
    return call(
        gradient_far_kernel,
        [IN_VMEM] * 6,
        [struct((rows, cols), f32), struct((rows, RANK), bf16)],
        2 * rows * wide * cols,
        2 * wide * cols,
        [pltpu.VMEM((rows, wide), bf16)],
    )(*halves, near, part, down_out, weight)


def lower_mask(rows):
    s = lax.broadcasted_iota(jnp.int32, (rows, rows), 0)
    t = lax.broadcasted_iota(jnp.int32, (rows, rows), 1)
    return s >= t


def lanes_of(h):
    return slice(h * HEAD_DIM, (h + 1) * HEAD_DIM)


def held_of(own_ref, back_ref, h):
    half = own_ref.shape[0]
    i = h % half
    if h < half:
        return jnp.where(first_core(), own_ref[i], back_ref[i])
    return jnp.where(first_core(), back_ref[i], own_ref[i])


def inside_kernel(qkv_ref, unread, scores_ref, raw_ref):
    mask = lower_mask(raw_ref.shape[0])
    for h in range(scores_ref.shape[0]):
        q, k, v = (qkv_ref[m, :, lanes_of(h)] for m in range(3))
        scores = jnp.where(mask, mm(q, k, NT), 0.0).astype(bf16)
        scores_ref[h] = scores
        raw_ref[:, lanes_of(h)] = mm(scores, v)


def inside_forward(qkv, unread):
    _, rows, cols = qkv.shape
    heads = cols // HEAD_DIM
    return call(
        inside_kernel,
        [IN_VMEM, UNREAD],
        [struct((heads, rows, rows), bf16), struct((rows, cols), f32)],
        4 * rows * cols * rows,
        6 * rows * cols,
    )(qkv, unread)


def halves_kernel(one_ref, three_ref, unread, top_ref, bottom_ref):
    half = top_ref.shape[0]
    top_ref[...] = one_ref[:half]
    bottom_ref[...] = three_ref[half:]


def halves(one, three, unread):
    rows, width = one.shape
    return call(
        halves_kernel,
        [IN_VMEM] * 2 + [UNREAD],
        [struct((rows // 2, width), bf16)] * 2,
        rows * width,
        4 * rows * width,
    )(one, three, unread)


def forward_kernel(
    qkv_ref, raw_ref, own_ref, back_ref, grad_ref, att_ref, draw_ref, mine_ref, given_ref, state
):
    for h in range(state.shape[0]):
        at = lanes_of(h)
        q = qkv_ref[0, :, at]
        raw = raw_ref[:, at] + mm(q, held_of(own_ref, back_ref, h))
        inverse = lax.rsqrt(jnp.mean(raw * raw, axis=-1, keepdims=True) + epsilon)
        normed = raw * inverse
        att_ref[:, at] = normed.astype(bf16)
        grad = grad_ref[:, at]
        along = jnp.mean(grad * normed, axis=-1, keepdims=True)
        draw = ((grad - normed * along) * inverse).astype(bf16)
        draw_ref[:, at] = draw
        state[h] = mm(q, draw, TN)
    split_states(state, mine_ref, given_ref)


def forward_heads(qkv, raw, held, grad):
    _, rows, cols = qkv.shape
    heads = cols // HEAD_DIM
    square = (HEAD_DIM, HEAD_DIM)
    return call(
        forward_kernel,
        [IN_VMEM] * 5,
        [
            struct((rows, cols), bf16),
            struct((rows, cols), bf16),
            struct((heads // 2,) + square, f32),
            struct((heads // 2,) + square, bf16),
        ],
        8 * rows * cols * HEAD_DIM,
        14 * rows * cols,
        [pltpu.VMEM((heads,) + square, f32)],
    )(qkv, raw, *held, grad)


def to_blocks(out_ref, base, rows):
    for b in range(rows.shape[1] // LANES):
        out_ref[base + b] = rows[:, b * LANES : (b + 1) * LANES]


def within_kernel(
    qkv_ref, scores_ref, own_ref, back_ref, draw_ref, att_ref, back_mid_ref, low_ref, up_ref,
    down_ref, unread, dq_ref, dk_ref, dv_ref, back_q_ref, mid_ref, early_ref,
):
    rows = draw_ref.shape[0]
    heads = scores_ref.shape[0]
    mask = lower_mask(rows)
    for h in range(heads):
        at = lanes_of(h)
        q, k, v = (qkv_ref[m, :, at] for m in range(3))
        draw = draw_ref[:, at]
        dscores = jnp.where(mask, mm(draw, v, NT), 0.0).astype(bf16)
        dq = mm(dscores, k) + mm(draw, held_of(own_ref, back_ref, h), NT)
        dq_ref[:, at] = dq.astype(bf16)
        dk_ref[:, at] = mm(dscores, q, TN)
        dv_ref[:, at] = mm(scores_ref[h], draw, TN)
    back_q_ref[...] = mm(dq_ref[...], up_ref[0], NT)
    mid_ref[...] = mm(att_ref[...], down_ref[...], NT)
    to_blocks(early_ref, 0, mm(back_mid_ref[...], att_ref[...], TN))
    to_blocks(early_ref, heads, mm(low_ref[:, :RANK], dq_ref[...], TN))


def within_block(qkv, scores, held, draw, att, back_mid, low, up, down_out, unread):
    _, rows, cols = qkv.shape
    heads = cols // HEAD_DIM
    return call(
        within_kernel,
        [IN_VMEM] * 10 + [UNREAD],
        [
            struct((rows, cols), bf16),
            struct((rows, cols), f32),
            struct((rows, cols), f32),
            struct((rows, RANK), f32),
            struct((rows, RANK), f32),
            struct((2 * heads, RANK, LANES), f32),
        ],
        4 * rows * cols * (4 * rows),
        18 * rows * cols,
    )(qkv, scores, *held, draw, att, back_mid, low, up, down_out, unread)


def across_kernel(
    qkv_ref, own_ref, back_ref, dk_ref, dv_ref, back_q_ref, mid_ref, up_ref, unread, out_ref, low_ref
):
    for h in range(out_ref.shape[2] // HEAD_DIM):
        at = lanes_of(h)
        held = held_of(own_ref, back_ref, h)
        out_ref[0, :, at] = (dk_ref[:, at] + mm(qkv_ref[2, :, at], held, NT)).astype(bf16)
        out_ref[1, :, at] = (dv_ref[:, at] + mm(qkv_ref[1, :, at], held)).astype(bf16)
    low_ref[:, :RANK] = back_q_ref[...].astype(bf16)
    low_ref[:, 3 * RANK :] = mid_ref[...].astype(bf16)
    for m in (1, 2):
        low_ref[:, m * RANK : (m + 1) * RANK] = mm(out_ref[m - 1], up_ref[m], NT).astype(bf16)


def across_blocks(qkv, held, dk, dv, back_q, mid, up, unread):
    _, rows, cols = qkv.shape
    return call(
        across_kernel,
        [IN_VMEM] * 8 + [UNREAD],
        [struct((2, rows, cols), bf16), struct((rows, 4 * RANK), bf16)],
        8 * rows * cols * HEAD_DIM,
        18 * rows * cols,
    )(qkv, *held, dk, dv, back_q, mid, up, unread)


def output_product(by, att_ref, weight_ref, width):
    chunk = pl.ds(pl.multiple_of(member(by) * width, width), width)
    return mm(att_ref[...], weight_ref[:, chunk])


def output_piece_kernel(shifts, att_ref, weight_ref, *refs):
    outs = refs[len(refs) - len(shifts) :]
    for by, out_ref in zip(shifts, outs):
        part = output_product(by, att_ref, weight_ref, out_ref.shape[1])
        out_ref[...] = part.astype(out_ref.dtype)


def output_pieces(shifts, att, weight, width, unread=()):
    rows, cols = att.shape
    return call(
        functools.partial(output_piece_kernel, shifts),
        [IN_VMEM] * 2 + [UNREAD] * len(unread),
        [struct((rows, width), bf16 if by else f32) for by in shifts],
        2 * rows * cols * width * len(shifts),
        2 * cols * width * len(shifts),
    )(att, weight, *unread)


def output_merge_kernel(own_ref, two_ref, one_ref, three_ref, unread, out_ref):
    total = own_ref[...]
    for ref in (two_ref, one_ref, three_ref):
        total = total + ref[...].astype(f32)
    out_ref[...] = total


def output_merge(own, parts, unread):
    return call(
        output_merge_kernel,
        [IN_VMEM] * 4 + [UNREAD],
        struct(own.shape, f32),
        2 * own.size,
        12 * own.size,
    )(own, *parts, unread)


def output_sum_kernel(merged_ref, low_ref, up_ref, unread, out_ref):
    total = merged_ref[...] + adapter_scale * mm(low_ref[:, 3 * RANK :], up_ref[...])
    out_ref[...] = total.astype(bf16)


def output_sum(merged, low, up, unread):
    rows, width = merged.shape
    return call(
        output_sum_kernel,
        [IN_VMEM] * 3 + [UNREAD],
        struct((rows, width), bf16),
        2 * rows * width * RANK,
        6 * rows * width,
    )(merged, low, up, unread)


def query_kernel(dq_ref, weight_ref, unread, out_ref):
    parts, _, width = out_ref.shape
    for p in range(parts):
        out_ref[p] = mm(dq_ref[...], weight_ref[0, p * width : (p + 1) * width], NT)


def query_part(dq, weight, width, unread):
    rows, cols = dq.shape
    parts = weight.shape[1] // width
    return call(
        query_kernel,
        [IN_VMEM] * 2 + [UNREAD],
        struct((parts, rows, width), f32),
        2 * rows * cols * width * parts,
        2 * cols * width * parts,
    )(dq, weight, unread)


def input_product(by, dkv_ref, dq_ref, weight_ref):
    total = dq_ref[member(by)]
    for m in range(2):
        total = total + mm(
            dkv_ref[m], chunk_rows(weight_ref, m + 1, by, total.shape[1]), NT
        )
    return total


def input_piece_kernel(by, dkv_ref, dq_ref, weight_ref, unread, out_ref):
    out_ref[...] = input_product(by, dkv_ref, dq_ref, weight_ref).astype(bf16)


def input_own_kernel(dkv_ref, dq_ref, weight_ref, unread, out_ref):
    out_ref[...] = input_product(0, dkv_ref, dq_ref, weight_ref)


def input_call(kernel, dkv, dq_parts, weight, out, *more):
    _, rows, cols = dkv.shape
    width = dq_parts.shape[2]
    return call(
        kernel,
        [IN_VMEM] * 3 + [UNREAD] * len(more),
        out,
        4 * rows * cols * width,
        4 * cols * width,
    )(dkv, dq_parts, weight, *more)


def input_sum_kernel(own_ref, two_ref, one_ref, three_ref, low_ref, down_ref, out_ref):
    total = own_ref[...] + adapter_scale * mm(low_ref[:, : 3 * RANK], down_ref[...])
    for ref in (two_ref, one_ref, three_ref):
        total = total + ref[...].astype(f32)
    out_ref[...] = total.astype(bf16)


def input_sum(own, parts, low, down_t):
    rows, width = own.shape
    return call(
        input_sum_kernel,
        [IN_VMEM] * 6,
        struct((rows, width), bf16),
        6 * rows * width * RANK,
        12 * rows * width,
    )(own, *parts, low, down_t)


def grads_kernel(
    back0, back2, back1, back3, tok_ref, cot_ref, low_ref, dkv_ref, early_ref,
    *refs,
):
    back_ref, mine_ref, given_ref, packed = refs[-4:]
    back = back0[...].astype(f32) + back2[...].astype(f32)
    back = (back + back1[...].astype(f32) + back3[...].astype(f32)).astype(bf16)
    back_ref[...] = back
    down = mm(back[:, : 3 * RANK], tok_ref[...], TN)
    up_out = mm(back[:, 3 * RANK :], cot_ref[...], TN)
    at = 0
    for m in range(3):
        to_blocks(packed, at, down[m * RANK : (m + 1) * RANK])
        at += tok_ref.shape[1] // LANES
    to_blocks(packed, at, up_out)
    at += cot_ref.shape[1] // LANES
    packed[at : at + early_ref.shape[0]] = early_ref[...]
    at += early_ref.shape[0]
    for m in (1, 2):
        to_blocks(packed, at, mm(low_ref[:, m * RANK : (m + 1) * RANK], dkv_ref[m - 1], TN))
        at += dkv_ref.shape[2] // LANES
    half = mine_ref.shape[0]
    first = first_core()
    mine_ref[...] = jnp.where(first, packed[:half], packed[half:])
    given_ref[...] = jnp.where(first, packed[half:], packed[:half]).astype(bf16)


def grads(backs, tokens, cot, low, dkv, early, unread):
    rows, width = tokens.shape
    cols = dkv.shape[2]
    half = 2 * (width + cols) // LANES
    return call(
        grads_kernel,
        [IN_VMEM] * 9 + [UNREAD] * len(unread),
        [
            struct(backs[0].shape, bf16),
            struct((half, RANK, LANES), f32),
            struct((half, RANK, LANES), bf16),
        ],
        2 * rows * RANK * (3 * width + 2 * cols),
        2 * dkv.size + 2 * tokens.size,
        [pltpu.VMEM((2 * half, RANK, LANES), f32)],
    )(*backs, tokens, cot, low, dkv, early, *unread)


def unpack_kernel(scale, own_ref, back_ref, down_ref, up_ref, down_out_ref, up_out_ref):
    half = own_ref.shape[0]
    at = 0

    def take(count):
        nonlocal at
        at += count
        first = first_core()
        blocks = []
        for b in range(at - count, at):
            own, back = own_ref[b % half], back_ref[b % half]
            block = jnp.where(first, own, back) if b < half else jnp.where(first, back, own)
            blocks.append(block.astype(f32))
        return scale * jnp.concatenate(blocks, axis=1)

    wide, heads = up_out_ref.shape[1] // LANES, down_out_ref.shape[1] // LANES
    for m in range(3):
        down_ref[m] = take(wide)
    up_out_ref[...] = take(wide)
    down_out_ref[...] = take(heads)
    for m in range(3):
        up_ref[m] = take(heads)


def unpack(own, back, scale, width, cols):
    return call(
        functools.partial(unpack_kernel, scale),
        [IN_VMEM] * 2,
        [
            struct((3, RANK, width), f32),
            struct((3, RANK, cols), f32),
            struct((RANK, cols), f32),
            struct((RANK, width), f32),
        ],
        own.size,
        12 * own.size,
    )(own, back)


def shift(array, by):
    n = lax.axis_size("head")
    return lax.ppermute(array, "head", [(i, (i + by) % n) for i in range(n)])


def from_head(array):
    return [shift(array, by) for by in (2, 1, 3)]


def swap_cores(array):
    n = lax.axis_size("ctx")
    return lax.ppermute(array, "ctx", [(i, i ^ 1) for i in range(n)])


def chip_place():
    n = lax.axis_size("ctx")
    chip = lax.axis_index("ctx") // 2
    side = {32: 4}[n]
    return lax.rem(chip, side), chip // side


def along(array, axis, by):
    n = lax.axis_size("ctx")
    side = {32: 4}[n]
    pairs = []
    for i in range(n):
        core, x, z = i % 2, (i // 2) % side, i // (2 * side)
        if axis == "x":
            x = (x + by) % side
        else:
            z = (z + by) % side
        pairs.append((i, (z * side + x) * 2 + core))
    return lax.ppermute(array, "ctx", pairs)


def from_axis(array, axis):
    return [along(array, axis, by) for by in (1, 3, 2)]


def pair_kernel(mine_ref, got_ref, out_ref):
    out_ref[...] = (mine_ref[...] + got_ref[...].astype(f32)).astype(bf16)


def before_sum(reverse, place, refs):
    total = jnp.zeros(refs[0].shape, f32)
    for by, ref in zip((1, 3, 2), refs):
        wanted = (place < by) if reverse else (place >= by)
        total = total + jnp.where(wanted, ref[...].astype(f32), 0.0)
    return total


def row_kernel(reverse, mine_ref, got_ref, one_ref, three_ref, two_ref, *refs):
    row_ref, before_ref = refs[-2:]
    others = (one_ref, three_ref, two_ref)
    total = mine_ref[...] + got_ref[...].astype(f32)
    for ref in others:
        total = total + ref[...].astype(f32)
    row_ref[...] = total.astype(bf16)
    before_ref[...] = before_sum(reverse, chip_place()[0], others)


def combine_kernel(
    reverse, mine_ref, got_ref, before_ref, one_ref, three_ref, two_ref, *refs
):
    own_ref, other_ref = refs[-2:]
    chip = before_ref[...] + before_sum(reverse, chip_place()[1], (one_ref, three_ref, two_ref))
    first = first_core() != reverse
    own_ref[...] = jnp.where(first, chip, chip + got_ref[...].astype(f32)).astype(bf16)
    other_ref[...] = jnp.where(first, chip + mine_ref[...], chip).astype(bf16)


def glue(kernel, operands, out_dtypes, unread=()):
    shape = operands[0].shape
    return call(
        kernel,
        [IN_VMEM] * len(operands) + [UNREAD] * len(unread),
        [struct(shape, dtype) for dtype in out_dtypes],
        operands[0].size,
        8 * operands[0].size,
    )(*operands, *unread)


def scan_pair(mine, given):
    got = swap_cores(given)
    return glue(pair_kernel, [mine, got], [bf16])[0], got


def scan_row(mine, got, arrived, reverse, during):
    row, before = glue(
        functools.partial(row_kernel, reverse), [mine, got] + arrived, [bf16, f32], during
    )
    return mine, got, row, before


def scan_rest(middle, arrived, reverse, during):
    mine, got, _, before = middle
    own, other = glue(
        functools.partial(combine_kernel, reverse),
        [mine, got, before] + arrived,
        [bf16, bf16],
        during,
    )
    return own, swap_cores(other)


def row_sum_kernel(count, mine_ref, *refs):
    total = mine_ref[...].astype(f32)
    for ref in refs[:count]:
        total = total + ref[...].astype(f32)
    refs[-1][...] = total.astype(bf16)


def sum_pair(mine, given):
    got = swap_cores(given)
    return glue(functools.partial(row_sum_kernel, 1), [mine, got], [bf16])[0], got


def sum_row(mine, got, arrived, during):
    return glue(
        functools.partial(row_sum_kernel, 4), [mine, got] + arrived, [bf16], during
    )[0]


def sum_rest(row, during):
    (total,) = glue(
        functools.partial(row_sum_kernel, 3), [row] + from_axis(row, "z"), [bf16], during
    )
    return total, swap_cores(total)


def on_device(
    tokens,
    query_key_value_weight,
    output_weight,
    input_down_weights,
    input_up_weights,
    output_down_weight,
    output_up_weight,
    cotangent,
):
    rows, width = tokens.shape
    cols = query_key_value_weight.shape[2]
    n = lax.axis_size("ctx")
    scale_factor = adapter_scale * (rows * n) ** (-0.5)
    down_t = input_down_weights.transpose(0, 2, 1).reshape(3 * RANK, width)
    down_out_t = output_down_weight.T

    weight = query_key_value_weight

    top, bottom = start(tokens, down_t)
    one_top, three_bottom = shift(top, 1), shift(bottom, 3)
    one_bottom, three_top = shift(bottom, 1), shift(top, 3)
    two = shift(one_top, 1), shift(three_bottom, 3)
    total = project_first(tokens, weight)
    total = project_next(1, (one_top, one_bottom), total, weight, width)
    total = project_next(3, (three_top, three_bottom), total, weight, width)
    cot_own = cotangent_parts(cotangent, output_up_weight, total)
    cot_one, cot_three = shift(cot_own, 1), shift(cot_own, 3)
    qkv, mine, given, low = project_last(
        two, total, (top, one_top, three_top), input_up_weights, weight, width
    )

    pair, got = scan_pair(mine, given)
    scores, raw = inside_forward(qkv, pair)
    arrived = from_axis(pair, "x")
    cot_top, cot_bottom = halves(cot_one, cot_three, arrived[0])
    cot_two = shift(cot_top, 1), shift(cot_bottom, 3)
    middle = scan_row(mine, got, arrived, False, [raw, cot_top])
    near_grad, back_near = gradient_near(
        [cot_own, cot_one, cot_three], output_weight, middle[2]
    )
    grad, back_mid = gradient_far(cot_two, near_grad, back_near, down_out_t, output_weight)
    held = scan_rest(middle, from_axis(middle[2], "z"), False, [near_grad])

    attended, d_raw, mine, given = forward_heads(qkv, raw, held, grad)
    pair, got = scan_pair(mine, given)
    (out_two,) = output_pieces((2,), attended, output_weight, width)
    out_own, out_one, out_three = output_pieces(
        (0, 1, 3), attended, output_weight, width, [pair]
    )
    out_got = [shift(part, by) for part, by in zip((out_two, out_one, out_three), (2, 1, 3))]
    middle = scan_row(mine, got, from_axis(pair, "x"), True, [out_own, out_got[0]])
    dq, dk_within, dv_within, back_q, mid, early = within_block(
        qkv,
        scores,
        held,
        d_raw,
        attended,
        back_mid,
        low,
        input_up_weights,
        down_out_t,
        middle[2],
    )
    dq_parts = query_part(dq, weight, width, middle[2])
    merged = output_merge(out_own, out_got, early)
    suffix = scan_rest(middle, from_axis(middle[2], "z"), True, [dq_parts])

    dkv, back_part = across_blocks(
        qkv, suffix, dk_within, dv_within, back_q, mid, input_up_weights, merged
    )
    back_got = from_head(back_part)
    piece, near = struct((rows, width), bf16), struct((rows, width), f32)

    def sent(by, unread):
        kernel = functools.partial(input_piece_kernel, by)
        part = input_call(kernel, dkv, dq_parts, weight, piece, unread)
        return part, shift(part, by)

    part_two, got_two = sent(2, back_got[0])
    part_one, got_one = sent(1, part_two)
    part_three, got_three = sent(3, part_one)
    back_low, mine, given = grads(
        [back_part] + back_got, tokens, cotangent, low, dkv, early, [part_three]
    )
    pair, got = sum_pair(mine, given)
    row = sum_row(mine, got, from_axis(pair, "x"), [got_two])
    grad_own = input_call(input_own_kernel, dkv, dq_parts, weight, near, row)
    output = output_sum(merged, back_low, output_up_weight, row)
    grad_got = [got_two, got_one, got_three]
    sums = sum_rest(row, [grad_own, output])
    input_grad = input_sum(grad_own, grad_got, back_low, down_t)
    grad_down_qkv, grad_up_qkv, grad_down_out, grad_up_out = unpack(
        *sums, scale_factor, width, cols
    )
    return (
        output,
        input_grad,
        grad_down_qkv.transpose(0, 2, 1),
        grad_up_qkv,
        grad_down_out.T,
        grad_up_out,
    )


def solution(mesh):
    return jax.shard_map(
        on_device,
        mesh=mesh,
        in_specs=(
            P("ctx", "head"),
            P(None, None, "head"),
            P("head", None),
            P(None, "head", None),
            P(None, None, "head"),
            P("head", None),
            P(None, "head"),
            P("ctx", "head"),
        ),
        out_specs=(
            P("ctx", "head"),
            P("ctx", "head"),
            P(None, "head", None),
            P(None, None, "head"),
            P("head", None),
            P(None, "head"),
        ),
        check_vma=False,
    )
```

```python
import functools

import jax
import jax.numpy as jnp
from jax import lax
from jax.experimental import pallas as pl
from jax.experimental.pallas import tpu as pltpu
from jax.sharding import PartitionSpec as P

HEAD_DIM = 128
RANK = 16
TILE = 256
LANES = 128
adapter_scale = 0.5
epsilon = 1e-06
bf16 = jnp.bfloat16
f32 = jnp.float32
HINT = 2 * 10**10
VMEM_BYTES = 12 * 2**20

NN = (((1,), (0,)), ((), ()))
NT = (((1,), (1,)), ((), ()))
TN = (((0,), (0,)), ((), ()))

IN_HBM = pl.BlockSpec(memory_space=pltpu.HBM)
IN_VMEM = pl.BlockSpec(memory_space=pltpu.VMEM)
UNREAD = pl.BlockSpec(memory_space=pl.ANY)


def mm(a, b, dims=NN):
    return lax.dot_general(a, b, dims, preferred_element_type=f32)


def struct(shape, dtype):
    return jax.ShapeDtypeStruct(shape, dtype)


def call(kernel, specs, out_shape, flops, moved, scratch=(), aliases=None):
    many = isinstance(out_shape, (list, tuple))
    return pl.pallas_call(
        kernel,
        in_specs=specs,
        out_specs=[IN_VMEM] * len(out_shape) if many else IN_VMEM,
        out_shape=out_shape,
        scratch_shapes=list(scratch),
        input_output_aliases=aliases or {},
        compiler_params=pltpu.CompilerParams(vmem_limit_bytes=VMEM_BYTES),
        cost_estimate=pl.CostEstimate(flops=flops, bytes_accessed=moved, transcendentals=0),
    )


def member(shift):
    return lax.rem(lax.axis_index("head") + shift + 4, 4)


def first_core():
    return lax.rem(lax.axis_index("ctx"), 2) == 0


def chunk_rows(weight_ref, m, shift, width):
    return weight_ref[m, pl.ds(pl.multiple_of(member(shift) * width, width), width)]


def start_kernel(tok_ref, down_ref, top_ref, bottom_ref):
    half = top_ref.shape[0]
    width = tok_ref.shape[1]
    top_ref[:, :width] = tok_ref[:half]
    bottom_ref[:, :width] = tok_ref[half:]
    small = mm(tok_ref[...], down_ref[...], NT)
    value = small.astype(bf16)
    rest = (small - value.astype(f32)).astype(bf16)
    pad = jnp.zeros((half, LANES - 6 * RANK), bf16)
    small = jnp.concatenate(
        [value[:half], rest[:half], pad, value[half:], rest[half:], pad], axis=1
    )
    top_ref[:, width:] = small
    bottom_ref[:, width:] = small


def start(tok, down_t):
    rows, width = tok.shape
    return call(
        start_kernel,
        [IN_VMEM] * 2,
        [struct((rows // 2, width + 2 * LANES), bf16)] * 2,
        HINT,
        6 * rows * width,
    )(tok, down_t)


def project_first_kernel(tok_ref, weight_ref, total_ref):
    for m in range(3):
        total_ref[m] = mm(tok_ref[...], chunk_rows(weight_ref, m, 0, tok_ref.shape[1]))


def project_first(tok, weight):
    rows, width = tok.shape
    cols = weight.shape[2]
    return call(
        project_first_kernel,
        [IN_VMEM] * 2,
        struct((3, rows, cols), f32),
        6 * rows * width * cols,
        6 * width * cols,
    )(tok, weight)


def joined(buffer, top_ref, bottom_ref):
    half = top_ref.shape[0]
    buffer[:half] = top_ref[:, : buffer.shape[1]]
    buffer[half:] = bottom_ref[:, : buffer.shape[1]]
    return buffer[...]


def project_next_kernel(by, top_ref, bottom_ref, sum_ref, weight_ref, total_ref, buffer):
    tok = joined(buffer, top_ref, bottom_ref)
    for m in range(3):
        total_ref[m] = sum_ref[m] + mm(tok, chunk_rows(weight_ref, m, -by, tok.shape[1]))


def project_next(by, halves, total, weight, width):
    _, rows, cols = total.shape
    return call(
        functools.partial(project_next_kernel, by),
        [IN_VMEM] * 4,
        struct((3, rows, cols), f32),
        6 * rows * width * cols,
        6 * width * cols,
        [pltpu.VMEM((rows, width), bf16)],
        {2: 0},
    )(*halves, total, weight)


def cotangent_kernel(cot_ref, out_up_ref, unread, out_ref):
    rows, width = cot_ref.shape
    out_ref[:, :width] = cot_ref[...]
    back = mm(cot_ref[...], out_up_ref[...], NT).astype(bf16)
    out_ref[:, width:] = jnp.concatenate(
        [back, jnp.zeros((rows, LANES - RANK), bf16)], axis=1
    )


def cotangent_parts(cot, out_up, unread):
    rows, width = cot.shape
    return call(
        cotangent_kernel,
        [IN_VMEM] * 2 + [UNREAD],
        struct((rows, width + LANES), bf16),
        2 * rows * width * RANK,
        4 * rows * width,
    )(cot, out_up, unread)


def split_states(state, mine_ref, given_ref):
    half = mine_ref.shape[0]
    first = first_core()
    for h in range(half):
        low, high = state[h], state[half + h]
        mine_ref[h] = jnp.where(first, low, high)
        given_ref[h] = jnp.where(first, high, low).astype(bf16)


def project_last_kernel(
    top_ref, bottom_ref, sum_ref, own_ref, one_ref, three_ref, up_ref, weight_ref,
    qkv_ref, mine_ref, given_ref, low_ref, state, buffer,
):
    tok = joined(buffer, top_ref, bottom_ref)
    half = top_ref.shape[0]
    width = tok.shape[1]
    low = sum(
        ref[:, width:].astype(f32) for ref in (own_ref, one_ref, three_ref, top_ref)
    )
    for at, part in ((slice(0, half), low[:, :LANES]), (slice(half, 2 * half), low[:, LANES:])):
        low_ref[at] = (part[:, : 3 * RANK] + part[:, 3 * RANK : 6 * RANK]).astype(bf16)
    for m in (1, 2, 0):
        total = sum_ref[m] + mm(tok, chunk_rows(weight_ref, m, -2, width))
        total = total + adapter_scale * mm(low_ref[:, m * RANK : (m + 1) * RANK], up_ref[m])
        qkv_ref[m] = total.astype(bf16)
    for h in range(state.shape[0]):
        at = slice(h * HEAD_DIM, (h + 1) * HEAD_DIM)
        state[h] = mm(qkv_ref[1, :, at], qkv_ref[2, :, at], TN)
    split_states(state, mine_ref, given_ref)


def project_last(halves, total, smalls, up, weight, width):
    _, rows, cols = total.shape
    heads = cols // HEAD_DIM
    square = (HEAD_DIM, HEAD_DIM)
    return call(
        project_last_kernel,
        [IN_VMEM] * 8,
        [
            struct((3, rows, cols), bf16),
            struct((heads // 2,) + square, f32),
            struct((heads // 2,) + square, bf16),
            struct((rows, 3 * RANK), bf16),
        ],
        6 * rows * width * cols,
        6 * width * cols,
        [pltpu.VMEM((heads,) + square, f32), pltpu.VMEM((rows, width), bf16)],
    )(*halves, total, *smalls, up, weight)


def gradient_near_kernel(cot0, cot1, cot3, unread, weight_ref, out_ref, back_ref):
    width = cot0.shape[1] - LANES
    refs = ((0, cot0), (1, cot1), (3, cot3))
    back_ref[...] = sum(ref[:, width : width + RANK].astype(f32) for _, ref in refs)
    total = jnp.zeros(out_ref.shape, f32)
    for by, ref in refs:
        chunk = pl.ds(pl.multiple_of(member(-by) * width, width), width)
        total = total + mm(ref[:, :width], weight_ref[:, chunk], NT)
    out_ref[...] = total


def gradient_near(cots, weight, unread):
    rows = cots[0].shape[0]
    cols, full = weight.shape
    return call(
        gradient_near_kernel,
        [IN_VMEM] * 3 + [UNREAD, IN_VMEM],
        [struct((rows, cols), f32), struct((rows, RANK), f32)],
        3 * rows * full * cols // 2,
        2 * full * cols,
    )(*cots, unread, weight)


def gradient_far_kernel(
    top_ref, bottom_ref, near_ref, part_ref, down_ref, weight_ref, out_ref, back_ref, buffer
):
    width = buffer.shape[1] - LANES
    joined(buffer, top_ref, bottom_ref)
    back = (part_ref[...] + buffer[:, width : width + RANK].astype(f32)).astype(bf16)
    back_ref[...] = back
    chunk = pl.ds(pl.multiple_of(member(-2) * width, width), width)
    total = near_ref[...] + mm(buffer[:, :width], weight_ref[:, chunk], NT)
    out_ref[...] = total + adapter_scale * mm(back, down_ref[...])


def gradient_far(halves, near, part, down_out, weight):
    rows, cols = near.shape
    wide = halves[0].shape[1]
    return call(
        gradient_far_kernel,
        [IN_VMEM] * 6,
        [struct((rows, cols), f32), struct((rows, RANK), bf16)],
        2 * rows * wide * cols,
        2 * wide * cols,
        [pltpu.VMEM((rows, wide), bf16)],
    )(*halves, near, part, down_out, weight)


def lower_mask(rows):
    s = lax.broadcasted_iota(jnp.int32, (rows, rows), 0)
    t = lax.broadcasted_iota(jnp.int32, (rows, rows), 1)
    return s >= t


def lanes_of(h):
    return slice(h * HEAD_DIM, (h + 1) * HEAD_DIM)


def held_of(own_ref, back_ref, h):
    half = own_ref.shape[0]
    i = h % half
    if h < half:
        return jnp.where(first_core(), own_ref[i], back_ref[i])
    return jnp.where(first_core(), back_ref[i], own_ref[i])


def inside_kernel(qkv_ref, unread, scores_ref, raw_ref):
    mask = lower_mask(raw_ref.shape[0])
    for h in range(scores_ref.shape[0]):
        q, k, v = (qkv_ref[m, :, lanes_of(h)] for m in range(3))
        scores = jnp.where(mask, mm(q, k, NT), 0.0).astype(bf16)
        scores_ref[h] = scores
        raw_ref[:, lanes_of(h)] = mm(scores, v)


def inside_forward(qkv, unread):
    _, rows, cols = qkv.shape
    heads = cols // HEAD_DIM
    return call(
        inside_kernel,
        [IN_VMEM, UNREAD],
        [struct((heads, rows, rows), bf16), struct((rows, cols), f32)],
        4 * rows * cols * rows,
        6 * rows * cols,
    )(qkv, unread)


def halves_kernel(one_ref, three_ref, unread, top_ref, bottom_ref):
    half = top_ref.shape[0]
    top_ref[...] = one_ref[:half]
    bottom_ref[...] = three_ref[half:]


def halves(one, three, unread):
    rows, width = one.shape
    return call(
        halves_kernel,
        [IN_VMEM] * 2 + [UNREAD],
        [struct((rows // 2, width), bf16)] * 2,
        rows * width,
        4 * rows * width,
    )(one, three, unread)


def forward_kernel(
    qkv_ref, raw_ref, own_ref, back_ref, grad_ref, att_ref, draw_ref, mine_ref, given_ref, state
):
    for h in range(state.shape[0]):
        at = lanes_of(h)
        q = qkv_ref[0, :, at]
        raw = raw_ref[:, at] + mm(q, held_of(own_ref, back_ref, h))
        inverse = lax.rsqrt(jnp.mean(raw * raw, axis=-1, keepdims=True) + epsilon)
        normed = raw * inverse
        att_ref[:, at] = normed.astype(bf16)
        grad = grad_ref[:, at]
        along = jnp.mean(grad * normed, axis=-1, keepdims=True)
        draw = ((grad - normed * along) * inverse).astype(bf16)
        draw_ref[:, at] = draw
        state[h] = mm(q, draw, TN)
    split_states(state, mine_ref, given_ref)


def forward_heads(qkv, raw, held, grad):
    _, rows, cols = qkv.shape
    heads = cols // HEAD_DIM
    square = (HEAD_DIM, HEAD_DIM)
    return call(
        forward_kernel,
        [IN_VMEM] * 5,
        [
            struct((rows, cols), bf16),
            struct((rows, cols), bf16),
            struct((heads // 2,) + square, f32),
            struct((heads // 2,) + square, bf16),
        ],
        8 * rows * cols * HEAD_DIM,
        14 * rows * cols,
        [pltpu.VMEM((heads,) + square, f32)],
    )(qkv, raw, *held, grad)


def to_blocks(out_ref, base, rows):
    for b in range(rows.shape[1] // LANES):
        out_ref[base + b] = rows[:, b * LANES : (b + 1) * LANES]


def within_kernel(
    qkv_ref, scores_ref, own_ref, back_ref, draw_ref, att_ref, back_mid_ref, low_ref, up_ref,
    down_ref, unread, dq_ref, dk_ref, dv_ref, back_q_ref, mid_ref, early_ref,
):
    rows = draw_ref.shape[0]
    heads = scores_ref.shape[0]
    mask = lower_mask(rows)
    for h in range(heads):
        at = lanes_of(h)
        q, k, v = (qkv_ref[m, :, at] for m in range(3))
        draw = draw_ref[:, at]
        dscores = jnp.where(mask, mm(draw, v, NT), 0.0).astype(bf16)
        dq = mm(dscores, k) + mm(draw, held_of(own_ref, back_ref, h), NT)
        dq_ref[:, at] = dq.astype(bf16)
        dk_ref[:, at] = mm(dscores, q, TN)
        dv_ref[:, at] = mm(scores_ref[h], draw, TN)
    back_q_ref[...] = mm(dq_ref[...], up_ref[0], NT)
    mid_ref[...] = mm(att_ref[...], down_ref[...], NT)
    to_blocks(early_ref, 0, mm(back_mid_ref[...], att_ref[...], TN))
    to_blocks(early_ref, heads, mm(low_ref[:, :RANK], dq_ref[...], TN))


def within_block(qkv, scores, held, draw, att, back_mid, low, up, down_out, unread):
    _, rows, cols = qkv.shape
    heads = cols // HEAD_DIM
    return call(
        within_kernel,
        [IN_VMEM] * 10 + [UNREAD],
        [
            struct((rows, cols), bf16),
            struct((rows, cols), f32),
            struct((rows, cols), f32),
            struct((rows, RANK), f32),
            struct((rows, RANK), f32),
            struct((2 * heads, RANK, LANES), f32),
        ],
        4 * rows * cols * (4 * rows),
        18 * rows * cols,
    )(qkv, scores, *held, draw, att, back_mid, low, up, down_out, unread)


def across_kernel(
    qkv_ref, own_ref, back_ref, dk_ref, dv_ref, back_q_ref, mid_ref, up_ref, unread, out_ref, low_ref
):
    for h in range(out_ref.shape[2] // HEAD_DIM):
        at = lanes_of(h)
        held = held_of(own_ref, back_ref, h)
        out_ref[0, :, at] = (dk_ref[:, at] + mm(qkv_ref[2, :, at], held, NT)).astype(bf16)
        out_ref[1, :, at] = (dv_ref[:, at] + mm(qkv_ref[1, :, at], held)).astype(bf16)
    low_ref[:, :RANK] = back_q_ref[...].astype(bf16)
    low_ref[:, 3 * RANK :] = mid_ref[...].astype(bf16)
    for m in (1, 2):
        low_ref[:, m * RANK : (m + 1) * RANK] = mm(out_ref[m - 1], up_ref[m], NT).astype(bf16)


def across_blocks(qkv, held, dk, dv, back_q, mid, up, unread):
    _, rows, cols = qkv.shape
    return call(
        across_kernel,
        [IN_VMEM] * 8 + [UNREAD],
        [struct((2, rows, cols), bf16), struct((rows, 4 * RANK), bf16)],
        8 * rows * cols * HEAD_DIM,
        18 * rows * cols,
    )(qkv, *held, dk, dv, back_q, mid, up, unread)


def output_product(by, att_ref, weight_ref, width):
    chunk = pl.ds(pl.multiple_of(member(by) * width, width), width)
    return mm(att_ref[...], weight_ref[:, chunk])


def output_piece_kernel(shifts, att_ref, weight_ref, *refs):
    outs = refs[len(refs) - len(shifts) :]
    for by, out_ref in zip(shifts, outs):
        part = output_product(by, att_ref, weight_ref, out_ref.shape[1])
        out_ref[...] = part.astype(out_ref.dtype)


def output_pieces(shifts, att, weight, width, unread=()):
    rows, cols = att.shape
    return call(
        functools.partial(output_piece_kernel, shifts),
        [IN_VMEM] * 2 + [UNREAD] * len(unread),
        [struct((rows, width), bf16 if by else f32) for by in shifts],
        2 * rows * cols * width * len(shifts),
        2 * cols * width * len(shifts),
    )(att, weight, *unread)


def output_merge_kernel(own_ref, two_ref, one_ref, three_ref, unread, out_ref):
    total = own_ref[...]
    for ref in (two_ref, one_ref, three_ref):
        total = total + ref[...].astype(f32)
    out_ref[...] = total


def output_merge(own, parts, unread):
    return call(
        output_merge_kernel,
        [IN_VMEM] * 4 + [UNREAD],
        struct(own.shape, f32),
        2 * own.size,
        12 * own.size,
    )(own, *parts, unread)


def output_sum_kernel(merged_ref, low_ref, up_ref, unread, out_ref):
    total = merged_ref[...] + adapter_scale * mm(low_ref[:, 3 * RANK :], up_ref[...])
    out_ref[...] = total.astype(bf16)


def output_sum(merged, low, up, unread):
    rows, width = merged.shape
    return call(
        output_sum_kernel,
        [IN_VMEM] * 3 + [UNREAD],
        struct((rows, width), bf16),
        2 * rows * width * RANK,
        6 * rows * width,
    )(merged, low, up, unread)


def query_kernel(dq_ref, weight_ref, unread, out_ref):
    parts, _, width = out_ref.shape
    for p in range(parts):
        out_ref[p] = mm(dq_ref[...], weight_ref[0, p * width : (p + 1) * width], NT)


def query_part(dq, weight, width, unread):
    rows, cols = dq.shape
    parts = weight.shape[1] // width
    return call(
        query_kernel,
        [IN_VMEM] * 2 + [UNREAD],
        struct((parts, rows, width), f32),
        2 * rows * cols * width * parts,
        2 * cols * width * parts,
    )(dq, weight, unread)


def input_product(by, dkv_ref, dq_ref, weight_ref):
    total = dq_ref[member(by)]
    for m in range(2):
        total = total + mm(
            dkv_ref[m], chunk_rows(weight_ref, m + 1, by, total.shape[1]), NT
        )
    return total


def input_piece_kernel(by, dkv_ref, dq_ref, weight_ref, unread, out_ref):
    out_ref[...] = input_product(by, dkv_ref, dq_ref, weight_ref).astype(bf16)


def input_own_kernel(dkv_ref, dq_ref, weight_ref, unread, out_ref):
    out_ref[...] = input_product(0, dkv_ref, dq_ref, weight_ref)


def input_call(kernel, dkv, dq_parts, weight, out, *more):
    _, rows, cols = dkv.shape
    width = dq_parts.shape[2]
    return call(
        kernel,
        [IN_VMEM] * 3 + [UNREAD] * len(more),
        out,
        4 * rows * cols * width,
        4 * cols * width,
    )(dkv, dq_parts, weight, *more)


def input_sum_kernel(own_ref, two_ref, one_ref, three_ref, low_ref, down_ref, out_ref):
    total = own_ref[...] + adapter_scale * mm(low_ref[:, : 3 * RANK], down_ref[...])
    for ref in (two_ref, one_ref, three_ref):
        total = total + ref[...].astype(f32)
    out_ref[...] = total.astype(bf16)


def input_sum(own, parts, low, down_t):
    rows, width = own.shape
    return call(
        input_sum_kernel,
        [IN_VMEM] * 6,
        struct((rows, width), bf16),
        6 * rows * width * RANK,
        12 * rows * width,
    )(own, *parts, low, down_t)


def grads_kernel(
    back0, back2, back1, back3, tok_ref, cot_ref, low_ref, dkv_ref, early_ref,
    *refs,
):
    back_ref, mine_ref, given_ref, packed = refs[-4:]
    back = back0[...].astype(f32) + back2[...].astype(f32)
    back = (back + back1[...].astype(f32) + back3[...].astype(f32)).astype(bf16)
    back_ref[...] = back
    down = mm(back[:, : 3 * RANK], tok_ref[...], TN)
    up_out = mm(back[:, 3 * RANK :], cot_ref[...], TN)
    at = 0
    for m in range(3):
        to_blocks(packed, at, down[m * RANK : (m + 1) * RANK])
        at += tok_ref.shape[1] // LANES
    to_blocks(packed, at, up_out)
    at += cot_ref.shape[1] // LANES
    packed[at : at + early_ref.shape[0]] = early_ref[...]
    at += early_ref.shape[0]
    for m in (1, 2):
        to_blocks(packed, at, mm(low_ref[:, m * RANK : (m + 1) * RANK], dkv_ref[m - 1], TN))
        at += dkv_ref.shape[2] // LANES
    half = mine_ref.shape[0]
    first = first_core()
    mine_ref[...] = jnp.where(first, packed[:half], packed[half:])
    given_ref[...] = jnp.where(first, packed[half:], packed[:half]).astype(bf16)


def grads(backs, tokens, cot, low, dkv, early, unread):
    rows, width = tokens.shape
    cols = dkv.shape[2]
    half = 2 * (width + cols) // LANES
    return call(
        grads_kernel,
        [IN_VMEM] * 9 + [UNREAD] * len(unread),
        [
            struct(backs[0].shape, bf16),
            struct((half, RANK, LANES), f32),
            struct((half, RANK, LANES), bf16),
        ],
        2 * rows * RANK * (3 * width + 2 * cols),
        2 * dkv.size + 2 * tokens.size,
        [pltpu.VMEM((2 * half, RANK, LANES), f32)],
    )(*backs, tokens, cot, low, dkv, early, *unread)


def unpack_kernel(scale, own_ref, back_ref, down_ref, up_ref, down_out_ref, up_out_ref):
    half = own_ref.shape[0]
    at = 0

    def take(count):
        nonlocal at
        at += count
        first = first_core()
        blocks = []
        for b in range(at - count, at):
            own, back = own_ref[b % half], back_ref[b % half]
            block = jnp.where(first, own, back) if b < half else jnp.where(first, back, own)
            blocks.append(block.astype(f32))
        return scale * jnp.concatenate(blocks, axis=1)

    wide, heads = up_out_ref.shape[1] // LANES, down_out_ref.shape[1] // LANES
    for m in range(3):
        down_ref[m] = take(wide)
    up_out_ref[...] = take(wide)
    down_out_ref[...] = take(heads)
    for m in range(3):
        up_ref[m] = take(heads)


def unpack(own, back, scale, width, cols):
    return call(
        functools.partial(unpack_kernel, scale),
        [IN_VMEM] * 2,
        [
            struct((3, RANK, width), f32),
            struct((3, RANK, cols), f32),
            struct((RANK, cols), f32),
            struct((RANK, width), f32),
        ],
        own.size,
        12 * own.size,
    )(own, back)


def shift(array, by):
    n = lax.axis_size("head")
    return lax.ppermute(array, "head", [(i, (i + by) % n) for i in range(n)])


def from_head(array):
    return [shift(array, by) for by in (2, 1, 3)]


def swap_cores(array):
    n = lax.axis_size("ctx")
    return lax.ppermute(array, "ctx", [(i, i ^ 1) for i in range(n)])


def chip_place():
    n = lax.axis_size("ctx")
    chip = lax.axis_index("ctx") // 2
    side = {32: 4}[n]
    return lax.rem(chip, side), chip // side


def along(array, axis, by):
    n = lax.axis_size("ctx")
    side = {32: 4}[n]
    pairs = []
    for i in range(n):
        core, x, z = i % 2, (i // 2) % side, i // (2 * side)
        if axis == "x":
            x = (x + by) % side
        else:
            z = (z + by) % side
        pairs.append((i, (z * side + x) * 2 + core))
    return lax.ppermute(array, "ctx", pairs)


def from_axis(array, axis):
    return [along(array, axis, by) for by in (1, 3, 2)]


def pair_kernel(mine_ref, got_ref, out_ref):
    out_ref[...] = (mine_ref[...] + got_ref[...].astype(f32)).astype(bf16)


def before_sum(reverse, place, refs):
    total = jnp.zeros(refs[0].shape, f32)
    for by, ref in zip((1, 3, 2), refs):
        wanted = (place < by) if reverse else (place >= by)
        total = total + jnp.where(wanted, ref[...].astype(f32), 0.0)
    return total


def row_kernel(reverse, mine_ref, got_ref, one_ref, three_ref, two_ref, *refs):
    row_ref, before_ref = refs[-2:]
    others = (one_ref, three_ref, two_ref)
    total = mine_ref[...] + got_ref[...].astype(f32)
    for ref in others:
        total = total + ref[...].astype(f32)
    row_ref[...] = total.astype(bf16)
    before_ref[...] = before_sum(reverse, chip_place()[0], others)


def combine_kernel(
    reverse, mine_ref, got_ref, before_ref, one_ref, three_ref, two_ref, *refs
):
    own_ref, other_ref = refs[-2:]
    chip = before_ref[...] + before_sum(reverse, chip_place()[1], (one_ref, three_ref, two_ref))
    first = first_core() != reverse
    own_ref[...] = jnp.where(first, chip, chip + got_ref[...].astype(f32)).astype(bf16)
    other_ref[...] = jnp.where(first, chip + mine_ref[...], chip).astype(bf16)


def glue(kernel, operands, out_dtypes, unread=()):
    shape = operands[0].shape
    return call(
        kernel,
        [IN_VMEM] * len(operands) + [UNREAD] * len(unread),
        [struct(shape, dtype) for dtype in out_dtypes],
        operands[0].size,
        8 * operands[0].size,
    )(*operands, *unread)


def scan_pair(mine, given):
    got = swap_cores(given)
    return glue(pair_kernel, [mine, got], [bf16])[0], got


def scan_row(mine, got, arrived, reverse, during):
    row, before = glue(
        functools.partial(row_kernel, reverse), [mine, got] + arrived, [bf16, f32], during
    )
    return mine, got, row, before


def scan_rest(middle, arrived, reverse, during):
    mine, got, _, before = middle
    own, other = glue(
        functools.partial(combine_kernel, reverse),
        [mine, got, before] + arrived,
        [bf16, bf16],
        during,
    )
    return own, swap_cores(other)


def row_sum_kernel(count, mine_ref, *refs):
    total = mine_ref[...].astype(f32)
    for ref in refs[:count]:
        total = total + ref[...].astype(f32)
    refs[-1][...] = total.astype(bf16)


def sum_pair(mine, given):
    got = swap_cores(given)
    return glue(functools.partial(row_sum_kernel, 1), [mine, got], [bf16])[0], got


def sum_row(mine, got, arrived, during):
    return glue(
        functools.partial(row_sum_kernel, 4), [mine, got] + arrived, [bf16], during
    )[0]


def sum_rest(row, during):
    (total,) = glue(
        functools.partial(row_sum_kernel, 3), [row] + from_axis(row, "z"), [bf16], during
    )
    return total, swap_cores(total)


def on_device(
    tokens,
    query_key_value_weight,
    output_weight,
    input_down_weights,
    input_up_weights,
    output_down_weight,
    output_up_weight,
    cotangent,
):
    rows, width = tokens.shape
    cols = query_key_value_weight.shape[2]
    n = lax.axis_size("ctx")
    scale_factor = adapter_scale * (rows * n) ** (-0.5)
    down_t = input_down_weights.transpose(0, 2, 1).reshape(3 * RANK, width)
    down_out_t = output_down_weight.T

    weight = query_key_value_weight

    top, bottom = start(tokens, down_t)
    one_top, three_bottom = shift(top, 1), shift(bottom, 3)
    one_bottom, three_top = shift(bottom, 1), shift(top, 3)
    two = shift(one_top, 1), shift(three_bottom, 3)
    total = project_first(tokens, weight)
    total = project_next(1, (one_top, one_bottom), total, weight, width)
    total = project_next(3, (three_top, three_bottom), total, weight, width)
    cot_own = cotangent_parts(cotangent, output_up_weight, total)
    cot_one, cot_three = shift(cot_own, 1), shift(cot_own, 3)
    qkv, mine, given, low = project_last(
        two, total, (top, one_top, three_top), input_up_weights, weight, width
    )

    pair, got = scan_pair(mine, given)
    arrived = from_axis(pair, "x")
    cot_top, cot_bottom = halves(cot_one, cot_three, arrived[0])
    cot_two = shift(cot_top, 1), shift(cot_bottom, 3)
    middle = scan_row(mine, got, arrived, False, [cot_top])
    scores, raw = inside_forward(qkv, middle[2])
    near_grad, back_near = gradient_near(
        [cot_own, cot_one, cot_three], output_weight, middle[2]
    )
    grad, back_mid = gradient_far(cot_two, near_grad, back_near, down_out_t, output_weight)
    held = scan_rest(middle, from_axis(middle[2], "z"), False, [near_grad, raw])

    attended, d_raw, mine, given = forward_heads(qkv, raw, held, grad)
    pair, got = scan_pair(mine, given)
    (out_two,) = output_pieces((2,), attended, output_weight, width)
    out_own, out_one, out_three = output_pieces(
        (0, 1, 3), attended, output_weight, width, [pair]
    )
    out_got = [shift(part, by) for part, by in zip((out_two, out_one, out_three), (2, 1, 3))]
    middle = scan_row(mine, got, from_axis(pair, "x"), True, [out_own, out_got[0]])
    dq, dk_within, dv_within, back_q, mid, early = within_block(
        qkv,
        scores,
        held,
        d_raw,
        attended,
        back_mid,
        low,
        input_up_weights,
        down_out_t,
        middle[2],
    )
    dq_parts = query_part(dq, weight, width, middle[2])
    merged = output_merge(out_own, out_got, early)
    suffix = scan_rest(middle, from_axis(middle[2], "z"), True, [dq_parts])

    dkv, back_part = across_blocks(
        qkv, suffix, dk_within, dv_within, back_q, mid, input_up_weights, merged
    )
    back_got = from_head(back_part)
    piece, near = struct((rows, width), bf16), struct((rows, width), f32)

    def sent(by, unread):
        kernel = functools.partial(input_piece_kernel, by)
        part = input_call(kernel, dkv, dq_parts, weight, piece, unread)
        return part, shift(part, by)

    part_two, got_two = sent(2, back_got[0])
    part_one, got_one = sent(1, part_two)
    part_three, got_three = sent(3, part_one)
    back_low, mine, given = grads(
        [back_part] + back_got, tokens, cotangent, low, dkv, early, [part_three]
    )
    pair, got = sum_pair(mine, given)
    row = sum_row(mine, got, from_axis(pair, "x"), [got_two])
    grad_own = input_call(input_own_kernel, dkv, dq_parts, weight, near, row)
    output = output_sum(merged, back_low, output_up_weight, row)
    grad_got = [got_two, got_one, got_three]
    sums = sum_rest(row, [grad_own, output])
    input_grad = input_sum(grad_own, grad_got, back_low, down_t)
    grad_down_qkv, grad_up_qkv, grad_down_out, grad_up_out = unpack(
        *sums, scale_factor, width, cols
    )
    return (
        output,
        input_grad,
        grad_down_qkv.transpose(0, 2, 1),
        grad_up_qkv,
        grad_down_out.T,
        grad_up_out,
    )


def solution(mesh):
    return jax.shard_map(
        on_device,
        mesh=mesh,
        in_specs=(
            P("ctx", "head"),
            P(None, None, "head"),
            P("head", None),
            P(None, "head", None),
            P(None, None, "head"),
            P("head", None),
            P(None, "head"),
            P("ctx", "head"),
        ),
        out_specs=(
            P("ctx", "head"),
            P("ctx", "head"),
            P(None, "head", None),
            P(None, None, "head"),
            P("head", None),
            P(None, "head"),
        ),
        check_vma=False,
    )
```
